32 devices in a mesh: row: 4 (over z), col: 8 (over y, x, core).
Axes of the slice: x: 2, y: 2, z: 4, core: 2. Of those that a mesh axis runs over, the one named last changes fastest.
Arguments:
- block_values: bfloat16 [4, 8, 256, 128, 128], P('row', 'col'), may hold values from -1.2 to 1.2
- block_rows: int32 [4, 8, 256], P('row', 'col'), may hold values from 0 to 103, as said below
- block_cols: int32 [4, 8, 256], P('row', 'col'), may hold values from 0 to 51, as said below
- start_vectors: bfloat16 [53248, 256], P(('row', 'col')), may hold values from -6 to 6
- center: float32 [1], replicated, may hold values from -0.5 to -0.1
- half_width: float32 [1], replicated, may hold values from 0.9 to 1.3
- row_counts: int32 [32], replicated, may hold values from 7 to 19, as said below
Outputs:
- relaid: bfloat16 [77824, 256], P(('row', 'col'))
The draws below stay inside these ranges and needn't reach their ends.
Inputs may be any that keep to these rules, and one draw needn't show every extreme that they name: `block_rows`: the first 13 entries of cell (r, c) are its diagonal blocks, at local row c * 13 + k; the rest are anywhere; positions may repeat, and repeated blocks add. `block_cols`: the first 13 entries of cell (r, c) are at local column r * 13 + k. `row_counts`: entries 2 i and 2 i + 1 sum to 26; entry 0 is larger than 13.
All inputs are finite; a program needn't handle non-finite values.
Results may differ from the reference program's by a relative error of at most 0.019.
Values may be sent and summed in bfloat16 or wider, within the bound.
No kernel may reach another device: no remote copies, remote signals or barrier semaphores. Data moves between devices by JAX's collectives and lax.ppermute only.
A program may use at most 192 MiB of HBM per device.

```python
import math
import jax
import jax.numpy as jnp
from jax import lax

ORB = 128
VECS = 256
BD = 13
NBD = 256
CAP = 19
ORDER = 53248
N_ROW = 4
N_COL = 8


def block_pattern(key):
    seeded = jax.random.fold_in(key, 7)
    first_key, second_key = jax.random.split(seeded)
    shape = (N_ROW, N_COL, NBD - BD)
    random_rows = jax.random.randint(first_key, shape, 0, N_COL * BD)
    random_cols = jax.random.randint(second_key, shape, 0, N_ROW * BD)
    diagonal = jnp.arange(BD, dtype=jnp.int32)
    diag_rows = jnp.broadcast_to(jnp.arange(N_COL, dtype=jnp.int32)[None, :, None] * BD + diagonal, (N_ROW, N_COL, BD))
    diag_cols = jnp.broadcast_to(jnp.arange(N_ROW, dtype=jnp.int32)[:, None, None] * BD + diagonal, (N_ROW, N_COL, BD))
    all_rows = jnp.concatenate([diag_rows, random_rows.astype(jnp.int32)], 2)
    all_cols = jnp.concatenate([diag_cols, random_cols.astype(jnp.int32)], 2)
    return (all_rows, all_cols)


def draw_block_rows(key, part):
    return block_pattern(key)[0].astype(jnp.int32)


def draw_block_cols(key, part):
    return block_pattern(key)[1].astype(jnp.int32)


def draw_block_values(key, part):
    seeded = jax.random.fold_in(key, 11)
    noise_key, onsite_key = jax.random.split(seeded)
    shape = (N_ROW, N_COL, NBD, ORB, ORB)
    spread = 0.35 / math.sqrt(ORB * NBD / BD)
    noise = jax.random.normal(noise_key, shape, jnp.float32) * spread
    onsite = jax.random.uniform(onsite_key, (N_ROW, N_COL, BD, ORB), jnp.float32, -1.0, 1.0)
    diag_part = onsite[..., :, None] * jnp.eye(ORB, dtype=jnp.float32)
    full = noise.at[:, :, :BD].add(diag_part)
    return full.astype(jnp.bfloat16)


def draw_row_counts(key, part):
    seeded = jax.random.fold_in(key, 13)
    delta_key, pick_key, sign_key, first_key = jax.random.split(seeded, 4)
    pair_count = N_ROW * N_COL // 2
    half_blocks = BD // 2
    deltas = jax.random.randint(delta_key, (pair_count,), -half_blocks, half_blocks + 1)
    first_delta = jax.random.randint(first_key, (), 1, half_blocks + 1)
    deltas = jnp.where(jnp.arange(pair_count) == 0, first_delta, deltas)
    chosen = jax.random.randint(pick_key, (), 0, pair_count)
    sign_value = jax.random.randint(sign_key, (), 0, 2) * 2 - 1
    sign_value = jnp.where(chosen == 0, 1, sign_value)
    deltas = jnp.where(jnp.arange(pair_count) == chosen, sign_value * half_blocks, deltas)
    counts = jnp.stack([BD + deltas, BD - deltas], axis=1).reshape(-1)
    return counts.astype(jnp.int32)


def steps_of(key, shape, shards, least, high):
    def one(axis_at, blocks):
        steps = jax.random.uniform(jax.random.fold_in(jax.random.fold_in(key, 6), axis_at), (blocks,), jnp.float32, least / len(shards), high / len(shards))
        return jnp.repeat(jnp.exp(steps), shape[axis_at] // blocks).reshape((-1,) + (1,) * (len(shape) - axis_at - 1))

    gain = one(*shards[0])
    for cut in shards[1:]:
        gain = gain * one(*cut)
    return gain


def normal_values(stream_key, shape, deviation, reach, cuts=(), held_as=jnp.bfloat16):
    gain = steps_of(stream_key, shape, cuts, -0.22, 0.18) if cuts else 1.0
    drawn = jax.random.normal(stream_key, shape, jnp.float32) * deviation * gain
    return jnp.minimum(jnp.maximum(drawn, -reach), reach).astype(held_as)


def setup_inputs(seed: int = 0) -> dict:
    streams_of = jax.random.split(jax.random.key(seed), 8)
    return {
        "block_values": draw_block_values(jax.random.fold_in(streams_of[7], 71), 0),
        "block_rows": draw_block_rows(jax.random.fold_in(streams_of[7], 71), 0),
        "block_cols": draw_block_cols(jax.random.fold_in(streams_of[7], 71), 0),
        "start_vectors": normal_values(streams_of[3], (ORDER, VECS), 1.0, 6.0, ((0, 32),)),
        "center": jnp.clip(jax.random.uniform(streams_of[4], (1,), jnp.float32, -0.5, -0.1), -0.5, -0.1),
        "half_width": jnp.clip(jax.random.uniform(streams_of[5], (1,), jnp.float32, 0.9, 1.3), 0.9, 1.3),
        "row_counts": draw_row_counts(jax.random.fold_in(streams_of[7], 71), 0),
    }


def cell_images(values, row_ids, col_ids, vector_blocks, grid_row):
    def one_cell(running, cell_items):
        cell_values, cell_rows, cell_cols, grid_col = cell_items
        global_cols = ((cell_cols // BD) * N_COL + grid_col) * BD + cell_cols % BD
        picked = vector_blocks[global_cols.astype(jnp.int32)]
        images = jnp.einsum("kij,kjv->kiv", cell_values.astype(jnp.float32), picked.astype(jnp.float32))
        cell_sum = jnp.zeros((N_COL * BD, ORB, VECS), jnp.float32).at[cell_rows].add(images)
        rounded = lax.optimization_barrier(cell_sum.astype(jnp.bfloat16))
        return running + rounded.astype(jnp.float32), None

    initial = jnp.zeros((N_COL * BD, ORB, VECS), jnp.float32)
    cell_items = (values[grid_row], row_ids[grid_row], col_ids[grid_row], jnp.arange(N_COL, dtype=jnp.int32))
    running, _ = lax.scan(one_cell, initial, cell_items)
    return running


def apply_operator(values, row_ids, col_ids, vectors):
    vector_blocks = vectors.reshape(BD * N_ROW * N_COL, ORB, VECS)
    pieces = [cell_images(values, row_ids, col_ids, vector_blocks, grid_row) for grid_row in range(N_ROW)]
    return jnp.concatenate(pieces, 0).reshape(ORDER, VECS)


def reference(block_values, block_rows, block_cols, start_vectors, center, half_width, row_counts):
    source = start_vectors.astype(jnp.float32)
    first_image = apply_operator(block_values, block_rows, block_cols, start_vectors)
    first_step = ((first_image - center[0] * source) / half_width[0]).astype(jnp.bfloat16)
    second_image = apply_operator(block_values, block_rows, block_cols, first_step)
    second_step = (2.0 * (second_image - center[0] * first_step.astype(jnp.float32)) / half_width[0] - source).astype(jnp.bfloat16)
    offsets = (jnp.cumsum(row_counts) - row_counts).astype(jnp.int32)
    padded = jnp.concatenate([second_step, jnp.zeros((CAP * ORB, VECS), jnp.bfloat16)], 0)

    def take_rows(offset, count):
        selected = lax.dynamic_slice_in_dim(padded, (offset * ORB).astype(jnp.int32), CAP * ORB, 0)
        live_rows = jnp.arange(CAP * ORB, dtype=jnp.int32)[:, None] < count * ORB
        return jnp.where(live_rows, selected, jnp.zeros_like(selected))

    relaid = jax.vmap(take_rows)(offsets, row_counts)
    return relaid.reshape(N_ROW * N_COL * CAP * ORB, VECS)
```

```python
import functools
import math

import jax
import jax.numpy as jnp
from jax import lax
from jax.experimental import pallas as pl
from jax.experimental.pallas import tpu as pltpu
from jax.sharding import PartitionSpec as P

UNROLL = 8
DEPTH = 4
LANES = 128


def sort_values(order, values):
    count = values.shape[0]

    def kernel(order_ref, values_ref, sorted_ref, sem):
        def send(slot, carry):
            pltpu.make_async_copy(
                values_ref.at[order_ref[slot]], sorted_ref.at[slot], sem
            ).start()
            return carry

        lax.fori_loop(0, count, send, 0)
        pltpu.make_async_copy(values_ref, sorted_ref, sem).wait()

    size = values.size * values.dtype.itemsize
    return pl.pallas_call(
        kernel,
        out_shape=jax.ShapeDtypeStruct(values.shape, values.dtype),
        in_specs=[pl.BlockSpec(memory_space=pltpu.SMEM), pl.BlockSpec(memory_space=pl.ANY)],
        out_specs=pl.BlockSpec(memory_space=pl.ANY),
        scratch_shapes=[pltpu.SemaphoreType.DMA],
        cost_estimate=pl.CostEstimate(flops=0, bytes_accessed=2 * size, transcendentals=0),
        name="sort_values",
    )(order, values)


def columns_of(vectors, low, width, after=None):
    rows = vectors.shape[0]
    cut = rows // 2 if rows % 32 == 0 else rows
    sizes = [cut, rows - cut] if cut < rows else [rows]

    def kernel(vectors_ref, *refs):
        out_refs = refs[len(after) :]
        row = 0
        for size, out_ref in zip(sizes, out_refs):
            out_ref[...] = vectors_ref[pl.ds(row, size), pl.ds(low, width)]
            row += size

    after = [] if after is None else list(after)
    return pl.pallas_call(
        kernel,
        out_shape=[jax.ShapeDtypeStruct((size, width), vectors.dtype) for size in sizes],
        in_specs=[pl.BlockSpec(memory_space=pltpu.VMEM)]
        + [pl.BlockSpec(memory_space=pl.ANY)] * len(after),
        out_specs=[pl.BlockSpec(memory_space=pltpu.VMEM)] * len(sizes),
        name="columns_of",
    )(vectors, *after)


def image_kernel(shape, bounds, rows, cols, values, *refs):
    first_piece, pieces, part_count, own, orbitals = shape
    parts = refs[:part_count]
    outs = refs[part_count : part_count + 2 * pieces]
    total, panel, slots, part_sems, slot_sems = refs[part_count + 2 * pieces :]
    start = bounds[first_piece]
    end = bounds[first_piece + pieces]
    first_group = start // UNROLL
    groups = (end + UNROLL - 1) // UNROLL - first_group

    def load(turn, slot):
        return pltpu.make_async_copy(
            values.at[pl.ds((first_group + turn) * UNROLL, UNROLL)],
            slots.at[slot],
            slot_sems.at[slot],
        )

    copies = []
    low = 0
    for index, part in enumerate(parts):
        copy = pltpu.make_async_copy(
            part, panel.at[pl.ds(low, part.shape[0])], part_sems.at[index]
        )
        copy.start()
        copies.append(copy)
        low += part.shape[0]
    for turn in range(DEPTH):
        @pl.when(turn < groups)
        def _():
            load(turn, turn).start()

    base = first_piece * 2 * own
    trash = pieces * 2 * own
    total[...] = jnp.zeros_like(total)
    for copy in copies:
        copy.wait()

    def step(turn, carry):
        slot = lax.rem(turn, DEPTH)
        load(turn, slot).wait()
        images = []
        for lane in range(UNROLL):
            entry = (first_group + turn) * UNROLL + lane
            picked = panel[pl.ds(pl.multiple_of(cols[entry] * orbitals, orbitals), orbitals), :]
            images.append(
                jnp.dot(slots[slot, lane], picked, preferred_element_type=jnp.float32)
            )
        for lane in range(UNROLL):
            entry = (first_group + turn) * UNROLL + lane
            inside = jnp.logical_and(entry >= start, entry < end)
            row = jnp.where(inside, rows[entry] - base, trash)
            place = pl.ds(pl.multiple_of(row * orbitals, orbitals), orbitals)
            total[place, :] += images[lane]

        @pl.when(turn + DEPTH < groups)
        def _():
            load(turn + DEPTH, slot).start()

        return carry

    lax.fori_loop(0, groups, step, 0)
    height = own * orbitals
    for index, out in enumerate(outs):
        out[...] = total[index * height : (index + 1) * height, :].astype(out.dtype)


def images_of(first_piece, pieces, bounds, rows, cols, values, parts, own):
    orbitals = values.shape[-1]
    width = parts[0].shape[1]
    panel_rows = sum(part.shape[0] for part in parts)
    out = jax.ShapeDtypeStruct((own * orbitals, width), jnp.bfloat16)
    entries = values.shape[0] * pieces // (bounds.shape[0] - 1)
    kernel = functools.partial(image_kernel, (first_piece, pieces, len(parts), own, orbitals))
    return pl.pallas_call(
        kernel,
        out_shape=[out] * (2 * pieces),
        in_specs=[pl.BlockSpec(memory_space=pltpu.SMEM)] * 3
        + [pl.BlockSpec(memory_space=pl.ANY)] * (1 + len(parts)),
        out_specs=[pl.BlockSpec(memory_space=pltpu.VMEM)] * (2 * pieces),
        scratch_shapes=[
            pltpu.VMEM(((pieces * 2 * own + 1) * orbitals, width), jnp.float32),
            pltpu.VMEM((panel_rows, width), jnp.bfloat16),
            pltpu.VMEM((DEPTH, UNROLL, orbitals, orbitals), values.dtype),
            pltpu.SemaphoreType.DMA((len(parts),)),
            pltpu.SemaphoreType.DMA((DEPTH,)),
        ],
        compiler_params=pltpu.CompilerParams(vmem_limit_bytes=48 << 20),
        cost_estimate=pl.CostEstimate(
            flops=entries * 8 * orbitals * orbitals * width,
            bytes_accessed=2 * (entries * orbitals * orbitals + panel_rows * width),
            transcendentals=0,
        ),
        name="images_of",
    )(bounds, rows, cols, values, *parts)


def ring_order(count):
    return [i for i in range(count) if i == 0 or i % 2] + [
        i for i in range(count - 1, 0, -1) if i and i % 2 == 0
    ]


def on_device(block_values, block_rows, block_cols, start_vectors, center, half_width, row_counts):
    orbitals = block_values.shape[-1]
    values = block_values.reshape(-1, orbitals, orbitals)
    row_ids = block_rows.reshape(-1)
    col_ids = block_cols.reshape(-1)
    entry_count = values.shape[0]
    own_rows, vec_count = start_vectors.shape
    own = own_rows // orbitals
    row_count = lax.axis_size("row")
    col_count = lax.axis_size("col")
    my_row = lax.axis_index("row")
    my_col = lax.axis_index("col")
    center_value = center[0]
    width_value = half_width[0]
    chip_count = col_count // 2

    order = ring_order(row_count)
    route = [(order[i], order[(i + 1) % row_count]) for i in range(row_count)]
    place_of = [order.index(i) for i in range(row_count)]

    def looked_up(table, index):
        result = jnp.zeros_like(index)
        for at, value in enumerate(table):
            result = jnp.where(index == at, value, result)
        return result

    with jax.named_scope("entry_order"):
        arrival = lax.rem(
            looked_up(place_of, my_row) - looked_up(place_of, col_ids // own) + row_count, row_count
        )
        panel_cols = arrival * own + col_ids % own
        relative = (row_ids // own) ^ my_col
        piece = chip_count - 1 - relative // 2
        out_rows = (piece * 2 + 1 - relative % 2) * own + row_ids % own
        number = jnp.arange(entry_count, dtype=jnp.int32)
        before = (out_rows[None, :] < out_rows[:, None]) | (
            (out_rows[None, :] == out_rows[:, None]) & (number[None, :] < number[:, None])
        )
        rank = jnp.sum(before.astype(jnp.int32), 1)
        at_rank = rank[None, :] == number[:, None]

        def ordered(items):
            return jnp.sum(jnp.where(at_rank, items[None, :], 0), 1).astype(jnp.int32)

        entry_order, rows, cols = ordered(number), ordered(out_rows), ordered(panel_cols)
        limits = jnp.arange(chip_count + 1, dtype=jnp.int32) * (2 * own)
        bounds = jnp.sum((out_rows[None, :] < limits[:, None]).astype(jnp.int32), 1)
        bounds = bounds.astype(jnp.int32)
    values = sort_values(entry_order, values)

    other_core = [(i, i ^ 1) for i in range(col_count)]
    if chip_count >= 4:
        groups = [(0, 1), (1, chip_count - 2), (chip_count - 1, 1)]
    else:
        groups = [(0, chip_count)]

    def gathered(parts):
        held = list(parts)
        arrived = [held]
        for _ in range(row_count - 1):
            held = [lax.ppermute(part, "row", route) for part in held]
            arrived.append(held)
        return arrived

    def summed(arrived):
        parts = [part for step in arrived for part in step]
        terms = None
        for first_piece, pieces in groups:
            outs = images_of(first_piece, pieces, bounds, rows, cols, values, parts, own)
            for index in range(pieces):
                chip = chip_count - 1 - first_piece - index
                partner = lax.ppermute(outs[2 * index], "col", other_core)
                both = outs[2 * index + 1].astype(jnp.float32) + partner.astype(jnp.float32)
                if chip:
                    both = lax.ppermute(
                        both.astype(jnp.bfloat16), "col",
                        [(i, i ^ 2 * chip) for i in range(col_count)],
                    ).astype(jnp.float32)
                terms = both if terms is None else terms + both
        return terms

    def pieces_of(array):
        cut = own_rows // 2 if own_rows % 32 == 0 else own_rows
        return [array[:cut], array[cut:]] if cut < own_rows else [array]

    lows = range(0, vec_count, LANES)
    first_arrived = []
    after = None
    for low in lows:
        arrived = gathered(columns_of(start_vectors, low, LANES, after))
        first_arrived.append(arrived)
        after = arrived[-1]
    firsts = []
    for low, arrived in zip(lows, first_arrived):
        source = start_vectors[:, low : low + LANES].astype(jnp.float32)
        first = ((summed(arrived) - center_value * source) / width_value).astype(jnp.bfloat16)
        firsts.append(first)
    second_arrived = [gathered(pieces_of(first)) for first in firsts]
    seconds = []
    for low, arrived, first in zip(lows, second_arrived, firsts):
        source = start_vectors[:, low : low + LANES].astype(jnp.float32)
        second = (
            2.0 * (summed(arrived) - center_value * first.astype(jnp.float32)) / width_value
            - source
        ).astype(jnp.bfloat16)
        seconds.append(second)
    second = jnp.concatenate(seconds, 1)

    device = my_row * col_count + my_col
    parity = device % 2
    even_count = row_counts[device - parity]
    own_count = row_counts[device]
    start_block = parity * even_count
    half_blocks = own // 2
    capacity = own + half_blocks
    edge_rows = jnp.where(
        parity == 0, second[own_rows - half_blocks * orbitals :], second[: half_blocks * orbitals]
    )
    partner = lax.ppermute(edge_rows, "col", other_core)
    window = jnp.where(
        parity == 0, jnp.concatenate([second, partner], 0), jnp.concatenate([partner, second], 0)
    )
    window_low = parity * (own - half_blocks)
    padded = jnp.concatenate([window, jnp.zeros((capacity * orbitals, vec_count), jnp.bfloat16)], 0)
    selected = lax.dynamic_slice_in_dim(
        padded, (start_block - window_low) * orbitals, capacity * orbitals, 0
    )
    live_rows = jnp.arange(capacity * orbitals, dtype=jnp.int32)[:, None] < own_count * orbitals
    return jnp.where(live_rows, selected, jnp.zeros_like(selected))


def solution(mesh):
    placed = (
        P("row", "col", None, None, None),
        P("row", "col", None),
        P("row", "col", None),
        P(("row", "col"), None),
        P(),
        P(),
        P(),
    )
    return jax.shard_map(
        on_device, mesh=mesh, in_specs=placed, out_specs=P(("row", "col"), None), check_vma=False
    )
```

```python
import functools
import math

import jax
import jax.numpy as jnp
from jax import lax
from jax.experimental import pallas as pl
from jax.experimental.pallas import tpu as pltpu
from jax.sharding import PartitionSpec as P

UNROLL = 16
MIB = 1 << 20
VMEM = pl.BlockSpec(memory_space=pltpu.VMEM)
SMEM = pl.BlockSpec(memory_space=pltpu.SMEM)
ANY = pl.BlockSpec(memory_space=pl.ANY)


def bytes_of(*shapes):
    return sum(math.prod(s.shape) * jnp.dtype(s.dtype).itemsize for s in shapes)


def params(need):
    return pltpu.CompilerParams(vmem_limit_bytes=need + 3 * MIB)


def resident(values):
    def kernel(values_ref, held_ref, sem):
        copy = pltpu.make_async_copy(values_ref, held_ref, sem)
        copy.start()
        copy.wait()

    return pl.pallas_call(
        kernel,
        out_shape=pltpu.VMEM(values.shape, values.dtype),
        in_specs=[ANY],
        out_specs=VMEM,
        scratch_shapes=[pltpu.SemaphoreType.DMA],
        compiler_params=pltpu.CompilerParams(vmem_limit_bytes=MIB),
        cost_estimate=pl.CostEstimate(
            flops=0, bytes_accessed=bytes_of(values), transcendentals=0
        ),
        name="resident",
    )(values)


def columns_of(vectors, row, rows, low, width, after):
    def kernel(vectors_ref, *refs):
        out_ref, sem = refs[-2:]
        copy = pltpu.make_async_copy(
            vectors_ref.at[pl.ds(row, rows), pl.ds(low, width)], out_ref, sem
        )
        copy.start()
        copy.wait()

    out = jax.ShapeDtypeStruct((rows, width), vectors.dtype)
    return pl.pallas_call(
        kernel,
        out_shape=out,
        in_specs=[ANY] * (1 + len(after)),
        out_specs=VMEM,
        scratch_shapes=[pltpu.SemaphoreType.DMA],
        compiler_params=params(bytes_of(out)),
        cost_estimate=pl.CostEstimate(
            flops=0, bytes_accessed=2 * bytes_of(out), transcendentals=0
        ),
        name="columns_of",
    )(vectors, *after)


def image_kernel(shape, bounds, order, rows, cols, values, *refs):
    first_piece, pieces, part_count, own, orbitals = shape
    parts = refs[:part_count]
    outs = refs[part_count : part_count + 2 * pieces]
    total, panel = refs[part_count + 2 * pieces :]
    start = bounds[first_piece]
    end = bounds[first_piece + pieces]
    base = first_piece * 2 * own
    trash = pieces * 2 * own
    low = 0
    for part in parts:
        panel[low : low + part.shape[0], :] = part[...]
        low += part.shape[0]
    total[...] = jnp.zeros_like(total)

    def step(turn, carry):
        images = []
        for lane in range(UNROLL):
            entry = start + turn * UNROLL + lane
            picked = panel[pl.ds(pl.multiple_of(cols[entry] * orbitals, orbitals), orbitals), :]
            images.append(
                jnp.dot(values[order[entry]], picked, preferred_element_type=jnp.float32)
            )
        for lane in range(UNROLL):
            entry = start + turn * UNROLL + lane
            row = jnp.where(entry < end, rows[entry] - base, trash)
            place = pl.ds(pl.multiple_of(row * orbitals, orbitals), orbitals)
            total[place, :] += images[lane]
        return carry

    lax.fori_loop(0, (end - start + UNROLL - 1) // UNROLL, step, 0)
    height = own * orbitals
    for index, out in enumerate(outs):
        out[...] = total[index * height : (index + 1) * height, :].astype(out.dtype)


def images_of(first_piece, pieces, tables, values, parts, own):
    orbitals = values.shape[-1]
    width = parts[0].shape[1]
    panel_rows = sum(part.shape[0] for part in parts)
    out = jax.ShapeDtypeStruct((own * orbitals, width), jnp.bfloat16)
    total = jax.ShapeDtypeStruct(((pieces * 2 * own + 1) * orbitals, width), jnp.float32)
    entries = values.shape[0] * pieces // (tables[0].shape[0] - 1)
    kernel = functools.partial(image_kernel, (first_piece, pieces, len(parts), own, orbitals))
    return pl.pallas_call(
        kernel,
        out_shape=[out] * (2 * pieces),
        in_specs=[SMEM] * 4 + [VMEM] * (1 + len(parts)),
        out_specs=[VMEM] * (2 * pieces),
        scratch_shapes=[
            pltpu.VMEM(total.shape, total.dtype),
            pltpu.VMEM((panel_rows, width), jnp.bfloat16),
        ],
        compiler_params=params(bytes_of(total, *parts, *parts) + 2 * pieces * bytes_of(out)),
        cost_estimate=pl.CostEstimate(
            flops=entries * 8 * orbitals * orbitals * width,
            bytes_accessed=2 * (entries * orbitals * orbitals + panel_rows * width),
            transcendentals=0,
        ),
        name="images_of",
    )(*tables, values, *parts)


def added(kept, arrived):
    def kernel(kept_ref, arrived_ref, out_ref):
        out_ref[...] = (
            kept_ref[...].astype(jnp.float32) + arrived_ref[...].astype(jnp.float32)
        ).astype(out_ref.dtype)

    return pl.pallas_call(
        kernel,
        out_shape=jax.ShapeDtypeStruct(kept.shape, kept.dtype),
        in_specs=[VMEM] * 2,
        out_specs=VMEM,
        compiler_params=params(3 * bytes_of(kept)),
        cost_estimate=pl.CostEstimate(
            flops=kept.size, bytes_accessed=3 * bytes_of(kept), transcendentals=0
        ),
        name="added",
    )(kept, arrived)


def first_update(terms, vectors, low, center, half_width, sizes):
    width = terms[0].shape[1]

    def kernel(center_ref, width_ref, vectors_ref, *refs):
        term_refs, out_refs = refs[: len(terms)], refs[len(terms) :]
        row = 0
        for size, out_ref in zip(sizes, out_refs):
            span = slice(row, row + size)
            image = term_refs[0][span, :].astype(jnp.float32)
            for term_ref in term_refs[1:]:
                image += term_ref[span, :].astype(jnp.float32)
            source = vectors_ref[span, low : low + width].astype(jnp.float32)
            out_ref[...] = ((image - center_ref[0] * source) / width_ref[0]).astype(out_ref.dtype)
            row += size

    need = bytes_of(*terms, vectors) + bytes_of(terms[0])
    return pl.pallas_call(
        kernel,
        out_shape=[jax.ShapeDtypeStruct((size, width), jnp.bfloat16) for size in sizes],
        in_specs=[SMEM] * 2 + [VMEM] * (1 + len(terms)),
        out_specs=[VMEM] * len(sizes),
        compiler_params=params(need),
        cost_estimate=pl.CostEstimate(flops=0, bytes_accessed=need, transcendentals=0),
        name="first_update",
    )(center, half_width, vectors, *terms)


def second_update(terms, firsts, vectors, low, center, half_width, edges, edge_size):
    rows, width = terms[0].shape

    def kernel(edges_ref, center_ref, width_ref, vectors_ref, *refs):
        term_refs = refs[: len(terms)]
        first_refs = refs[len(terms) : len(terms) + len(firsts)]
        out_ref, edge_ref = refs[len(terms) + len(firsts) :]
        row = 0
        for first_ref in first_refs:
            span = slice(row, row + first_ref.shape[0])
            image = term_refs[0][span, :].astype(jnp.float32)
            for term_ref in term_refs[1:]:
                image += term_ref[span, :].astype(jnp.float32)
            source = vectors_ref[span, low : low + width].astype(jnp.float32)
            first = first_ref[...].astype(jnp.float32)
            out_ref[span, :] = (
                2.0 * (image - center_ref[0] * first) / width_ref[0] - source
            ).astype(out_ref.dtype)
            row += first_ref.shape[0]
        edge_ref[...] = out_ref[pl.ds(pl.multiple_of(edges_ref[0], 16), edge_size), :]

    need = bytes_of(*terms, *firsts, vectors) + 2 * bytes_of(terms[0])
    return pl.pallas_call(
        kernel,
        out_shape=[
            jax.ShapeDtypeStruct((rows, width), jnp.bfloat16),
            jax.ShapeDtypeStruct((edge_size, width), jnp.bfloat16),
        ],
        in_specs=[SMEM] * 3 + [VMEM] * (1 + len(terms) + len(firsts)),
        out_specs=[VMEM] * 2,
        compiler_params=params(need),
        cost_estimate=pl.CostEstimate(flops=0, bytes_accessed=need, transcendentals=0),
        name="second_update",
    )(edges, center, half_width, vectors, *terms, *firsts)


def relaid_rows(seconds, partners, edges, own, capacity, orbitals):
    width = seconds[0].shape[1]
    count = len(seconds)
    edge_size = partners[0].shape[0]

    def kernel(edges_ref, *refs):
        out_ref, window = refs[-2:]
        for index in range(count):
            window[pl.ds(pl.multiple_of(edges_ref[1], 16), own * orbitals), :] = refs[index][...]
            window[pl.ds(pl.multiple_of(edges_ref[2], 16), edge_size), :] = refs[count + index][...]
            for block in range(capacity):
                lane = slice(index * width, (index + 1) * width)
                span = slice(block * orbitals, (block + 1) * orbitals)

                @pl.when(block < edges_ref[4])
                def _():
                    row = pl.multiple_of(edges_ref[3] + block * orbitals, 16)
                    out_ref[span, lane] = window[pl.ds(row, orbitals), :]

                @pl.when(block >= edges_ref[4])
                def _():
                    out_ref[span, lane] = jnp.zeros((orbitals, width), out_ref.dtype)

    out = jax.ShapeDtypeStruct((capacity * orbitals, count * width), jnp.bfloat16)
    need = 2 * bytes_of(out) + bytes_of(*seconds, *partners)
    return pl.pallas_call(
        kernel,
        out_shape=out,
        in_specs=[SMEM] + [VMEM] * (2 * count),
        out_specs=VMEM,
        scratch_shapes=[pltpu.VMEM((own * orbitals + edge_size, width), jnp.bfloat16)],
        compiler_params=params(need),
        cost_estimate=pl.CostEstimate(flops=0, bytes_accessed=need, transcendentals=0),
        name="relaid_rows",
    )(edges, *seconds, *partners)


def ring_order(count):
    return [i for i in range(count) if i == 0 or i % 2] + [
        i for i in range(count - 1, 0, -1) if i and i % 2 == 0
    ]


def on_device(block_values, block_rows, block_cols, start_vectors, center, half_width, row_counts):
    orbitals = block_values.shape[-1]
    values = block_values.reshape(-1, orbitals, orbitals)
    row_ids = block_rows.reshape(-1)
    col_ids = block_cols.reshape(-1)
    entry_count = values.shape[0]
    own_rows, vec_count = start_vectors.shape
    own = own_rows // orbitals
    row_count = lax.axis_size("row")
    col_count = lax.axis_size("col")
    my_row = lax.axis_index("row")
    my_col = lax.axis_index("col")
    chip_count = col_count // 2

    order = ring_order(row_count)
    route = [(order[i], order[(i + 1) % row_count]) for i in range(row_count)]
    place_of = [order.index(i) for i in range(row_count)]

    def looked_up(table, index):
        result = jnp.zeros_like(index)
        for at, value in enumerate(table):
            result = jnp.where(index == at, value, result)
        return result

    with jax.named_scope("entry_order"):
        arrival = lax.rem(
            looked_up(place_of, my_row) - looked_up(place_of, col_ids // own) + row_count, row_count
        )
        panel_cols = arrival * own + col_ids % own
        relative = (row_ids // own) ^ my_col
        piece = chip_count - 1 - relative // 2
        out_rows = (piece * 2 + 1 - relative % 2) * own + row_ids % own
        number = jnp.arange(entry_count, dtype=jnp.int32)
        before = (out_rows[None, :] < out_rows[:, None]) | (
            (out_rows[None, :] == out_rows[:, None]) & (number[None, :] < number[:, None])
        )
        rank = jnp.sum(before.astype(jnp.int32), 1)
        at_rank = rank[None, :] == number[:, None]

        def ordered(items):
            return jnp.sum(jnp.where(at_rank, items[None, :], 0), 1).astype(jnp.int32)

        room = (0, UNROLL)
        entry_order = jnp.pad(ordered(number), room)
        rows = jnp.pad(ordered(out_rows), room)
        cols = jnp.pad(ordered(panel_cols), room)
        limits = jnp.arange(chip_count + 1, dtype=jnp.int32) * (2 * own)
        bounds = jnp.sum((out_rows[None, :] < limits[:, None]).astype(jnp.int32), 1)
        bounds = bounds.astype(jnp.int32)
        tables = (bounds, entry_order, rows, cols)
    values = resident(values)

    other_core = [(i, i ^ 1) for i in range(col_count)]
    if chip_count >= 4:
        groups = [(0, 1), (1, chip_count - 2), (chip_count - 1, 1)]
    else:
        groups = [(0, chip_count)]
    lanes = 128 if vec_count % 128 == 0 else vec_count
    lows = range(0, vec_count, lanes)
    cut = own_rows // 2 if own_rows % 32 == 0 else own_rows
    sizes = [cut, own_rows - cut] if cut < own_rows else [own_rows]

    def gathered(parts):
        held = list(parts)
        arrived = [held]
        for _ in range(row_count - 1):
            held = [lax.ppermute(part, "row", route) for part in held]
            arrived.append(held)
        return arrived

    def terms_of(arrived):
        parts = [part for step in arrived for part in step]
        terms = []
        for first_piece, pieces in groups:
            outs = images_of(first_piece, pieces, tables, values, parts, own)
            for index in range(pieces):
                chip = chip_count - 1 - first_piece - index
                kept = outs[2 * index + 1]
                partner = lax.ppermute(outs[2 * index], "col", other_core)
                if chip:
                    chips = [(i, i ^ 2 * chip) for i in range(col_count)]
                    terms.append(lax.ppermute(added(kept, partner), "col", chips))
                else:
                    terms += [kept, partner]
        return terms

    half_blocks = own // 2
    capacity = own + half_blocks
    edge_size = half_blocks * orbitals
    device = my_row * col_count + my_col
    parity = device % 2
    even_count = row_counts[device - parity]
    edges = jnp.stack(
        [
            (1 - parity) * (own_rows - edge_size),
            parity * edge_size,
            (1 - parity) * own_rows,
            parity * (even_count - (own - half_blocks)) * orbitals,
            row_counts[device],
        ]
    ).astype(jnp.int32)

    first_arrived = []
    after = [[] for _ in sizes]
    for low in lows:
        parts = [
            columns_of(start_vectors, index * cut, size, low, lanes, after[index])
            for index, size in enumerate(sizes)
        ]
        first_arrived.append(gathered(parts))
        after = [[part] for part in first_arrived[-1][-1]]
    firsts = [
        first_update(terms_of(arrived), start_vectors, low, center, half_width, sizes)
        for low, arrived in zip(lows, first_arrived)
    ]
    seconds, partners = [], []
    for low, first in zip(lows, firsts):
        terms = terms_of(gathered(first))
        second, edge = second_update(
            terms, first, start_vectors, low, center, half_width, edges, edge_size
        )
        seconds.append(second)
        partners.append(lax.ppermute(edge, "col", other_core))
    return relaid_rows(seconds, partners, edges, own, capacity, orbitals)


def solution(mesh):
    placed = (
        P("row", "col", None, None, None),
        P("row", "col", None),
        P("row", "col", None),
        P(("row", "col"), None),
        P(),
        P(),
        P(),
    )
    return jax.shard_map(
        on_device, mesh=mesh, in_specs=placed, out_specs=P(("row", "col"), None), check_vma=False
    )
```

```python
import functools
import math

import jax
import jax.numpy as jnp
from jax import lax
from jax.experimental import pallas as pl
from jax.experimental.pallas import tpu as pltpu
from jax.sharding import PartitionSpec as P

UNROLL = 32
EDGES = 5
MIB = 1 << 20
VMEM = pl.BlockSpec(memory_space=pltpu.VMEM)
SMEM = pl.BlockSpec(memory_space=pltpu.SMEM)
ANY = pl.BlockSpec(memory_space=pl.ANY)
HBM = pl.BlockSpec(memory_space=pltpu.HBM)


def bytes_of(*shapes):
    return sum(math.prod(s.shape) * jnp.dtype(s.dtype).itemsize for s in shapes)


def params(need):
    return pltpu.CompilerParams(vmem_limit_bytes=need + 3 * MIB)


def resident(values, after):
    def kernel(values_ref, *refs):
        held_ref, sem = refs[-2:]
        copy = pltpu.make_async_copy(values_ref, held_ref, sem)
        copy.start()
        copy.wait()

    return pl.pallas_call(
        kernel,
        out_shape=pltpu.VMEM(values.shape, values.dtype),
        in_specs=[HBM] + [ANY] * len(after),
        out_specs=VMEM,
        scratch_shapes=[pltpu.SemaphoreType.DMA],
        compiler_params=pltpu.CompilerParams(vmem_limit_bytes=MIB),
        cost_estimate=pl.CostEstimate(
            flops=0, bytes_accessed=bytes_of(values), transcendentals=0
        ),
        name="resident",
    )(values, *after)


def columns_of(vectors, row, rows, low, width, after):
    def kernel(vectors_ref, *refs):
        out_ref, sem = refs[-2:]
        copy = pltpu.make_async_copy(
            vectors_ref.at[pl.ds(row, rows), pl.ds(low, width)], out_ref, sem
        )
        copy.start()
        copy.wait()

    out = jax.ShapeDtypeStruct((rows, width), vectors.dtype)
    return pl.pallas_call(
        kernel,
        out_shape=out,
        in_specs=[HBM] + [ANY] * len(after),
        out_specs=VMEM,
        scratch_shapes=[pltpu.SemaphoreType.DMA],
        compiler_params=params(bytes_of(out)),
        cost_estimate=pl.CostEstimate(
            flops=0, bytes_accessed=2 * bytes_of(out), transcendentals=0
        ),
        name="columns_of",
    )(vectors, *after)


def add_images(bounds, order, rows, cols, values, panel, total, phase, low_col):
    orbitals = values.shape[-1]
    trash = total.shape[0] // orbitals - 1
    start = bounds[EDGES + phase]
    end = bounds[EDGES + phase + 1]

    def step(turn, carry):
        images = []
        for lane in range(UNROLL):
            entry = start + turn * UNROLL + lane
            col = jnp.where(entry < end, cols[entry] - low_col, 0)
            picked = panel[pl.ds(pl.multiple_of(col * orbitals, orbitals), orbitals), :]
            images.append(
                jnp.dot(values[order[entry]], picked, preferred_element_type=jnp.float32)
            )
        for lane in range(UNROLL):
            entry = start + turn * UNROLL + lane
            row = jnp.where(entry < end, rows[entry], trash)
            place = pl.ds(pl.multiple_of(row * orbitals, orbitals), orbitals)
            total[place, :] += images[lane]
        return carry

    lax.fori_loop(0, (end - start + UNROLL - 1) // UNROLL, step, 0)


def fill(panel, parts):
    low = 0
    for part in parts:
        panel[low : low + part.shape[0], :] = part[...]
        low += part.shape[0]


def early_images(out_blocks, tables, values, parts):
    orbitals = values.shape[-1]
    width = parts[0].shape[1]
    panel_rows = sum(part.shape[0] for part in parts)
    total = ((out_blocks + 1) * orbitals, width)

    def kernel(bounds, order, rows, cols, values, *refs):
        total_ref, panel = refs[-2:]
        fill(panel, refs[:-2])
        total_ref[...] = jnp.zeros_like(total_ref)
        add_images(bounds, order, rows, cols, values, panel, total_ref, 0, 0)

    return pl.pallas_call(
        kernel,
        out_shape=pltpu.VMEM(total, jnp.float32),
        in_specs=[SMEM] * 4 + [VMEM] * (1 + len(parts)),
        out_specs=VMEM,
        scratch_shapes=[pltpu.VMEM((panel_rows, width), jnp.bfloat16)],
        compiler_params=params(bytes_of(*parts, *parts)),
        name="early_images",
    )(*tables, values, *parts)


def last_images(counts, low_col, tables, values, early, parts):
    orbitals = values.shape[-1]
    width = parts[0].shape[1]
    panel_rows = sum(part.shape[0] for part in parts)
    height = (early.shape[0] - orbitals) // (2 * sum(counts))
    outs = [
        jax.ShapeDtypeStruct((count * height, width), jnp.bfloat16)
        for count in counts
        for _ in range(2)
    ]

    def kernel(bounds, order, rows, cols, values, early, *refs):
        part_refs, out_refs = refs[: len(parts)], refs[len(parts) + 1 : -1]
        total, panel = refs[len(parts)], refs[-1]
        fill(panel, part_refs)
        add_images(bounds, order, rows, cols, values, panel, total, 1, low_col)
        low = 0
        for count, *pair in zip(counts, out_refs[::2], out_refs[1::2]):
            for piece in range(count):
                for out in pair:
                    out[piece * height : (piece + 1) * height, :] = total[
                        low : low + height, :
                    ].astype(out.dtype)
                    low += height

    return pl.pallas_call(
        kernel,
        out_shape=[pltpu.VMEM(early.shape, jnp.float32), *outs],
        in_specs=[SMEM] * 4 + [VMEM] * (2 + len(parts)),
        out_specs=[VMEM] * (1 + len(outs)),
        scratch_shapes=[pltpu.VMEM((panel_rows, width), jnp.bfloat16)],
        input_output_aliases={5: 0},
        compiler_params=params(bytes_of(*parts, *parts, *outs)),
        name="last_images",
    )(*tables, values, early, *parts)[1:]


def summed(specs):
    flat = [array for segments in specs for _, pairs in segments for array, _ in pairs]

    def kernel(*refs):
        out_refs = refs[len(flat) :]
        at = 0
        for segments, out_ref in zip(specs, out_refs):
            row = 0
            for size, pairs in segments:
                total = image_rows(refs[at : at + len(pairs)], pairs, size)
                at += len(pairs)
                out_ref[row : row + size, :] = total.astype(out_ref.dtype)
                row += size

    width = flat[0].shape[1]
    outs = [
        jax.ShapeDtypeStruct((sum(size for size, _ in segments), width), flat[0].dtype)
        for segments in specs
    ]
    need = bytes_of(*flat, *outs)
    return pl.pallas_call(
        kernel,
        out_shape=outs,
        in_specs=[VMEM] * len(flat),
        out_specs=[VMEM] * len(outs),
        compiler_params=params(need),
        cost_estimate=pl.CostEstimate(flops=0, bytes_accessed=need, transcendentals=0),
        name="summed",
    )(*flat)


def image_rows(refs, pairs, size):
    image = None
    for ref, (_, low) in zip(refs, pairs):
        term = ref[low : low + size, :].astype(jnp.float32)
        image = term if image is None else image + term
    return image


def first_update(terms, vectors, low, center, half_width):
    flat = [array for _, pairs in terms for array, _ in pairs]
    width = flat[0].shape[1]

    def kernel(center_ref, width_ref, vectors_ref, *refs):
        out_refs = refs[len(flat) :]
        row, at = 0, 0
        for (size, pairs), out_ref in zip(terms, out_refs):
            image = image_rows(refs[at : at + len(pairs)], pairs, size)
            at += len(pairs)
            source = vectors_ref[row : row + size, low : low + width].astype(jnp.float32)
            out_ref[...] = ((image - center_ref[0] * source) / width_ref[0]).astype(out_ref.dtype)
            row += size

    need = bytes_of(*flat, vectors)
    return pl.pallas_call(
        kernel,
        out_shape=[jax.ShapeDtypeStruct((size, width), jnp.bfloat16) for size, _ in terms],
        in_specs=[SMEM] * 2 + [VMEM] * (1 + len(flat)),
        out_specs=[VMEM] * len(terms),
        compiler_params=params(need),
        cost_estimate=pl.CostEstimate(flops=0, bytes_accessed=need, transcendentals=0),
        name="first_update",
    )(center, half_width, vectors, *flat)


def second_update(terms, firsts, vectors, low, center, half_width, tables, edge_size):
    flat = [array for _, pairs in terms for array, _ in pairs]
    rows = sum(size for size, _ in terms)
    width = flat[0].shape[1]

    def kernel(edges_ref, center_ref, width_ref, vectors_ref, *refs):
        first_refs = refs[len(flat) : len(flat) + len(firsts)]
        out_ref, edge_ref = refs[-2:]
        row, at = 0, 0
        for (size, pairs), first_ref in zip(terms, first_refs):
            image = image_rows(refs[at : at + len(pairs)], pairs, size)
            at += len(pairs)
            source = vectors_ref[row : row + size, low : low + width].astype(jnp.float32)
            first = first_ref[...].astype(jnp.float32)
            out_ref[row : row + size, :] = (
                2.0 * (image - center_ref[0] * first) / width_ref[0] - source
            ).astype(out_ref.dtype)
            row += size
        edge_ref[...] = out_ref[pl.ds(pl.multiple_of(edges_ref[0], 16), edge_size), :]

    need = bytes_of(*flat, *firsts, vectors) + 4 * rows * width
    return pl.pallas_call(
        kernel,
        out_shape=[
            jax.ShapeDtypeStruct((rows, width), jnp.bfloat16),
            jax.ShapeDtypeStruct((edge_size, width), jnp.bfloat16),
        ],
        in_specs=[SMEM] * 3 + [VMEM] * (1 + len(flat) + len(firsts)),
        out_specs=[VMEM] * 2,
        compiler_params=params(need),
        cost_estimate=pl.CostEstimate(flops=0, bytes_accessed=need, transcendentals=0),
        name="second_update",
    )(tables[0], center, half_width, vectors, *flat, *firsts)


def relaid_half(relaid, second, partner, edges, low, shape, own, orbitals):
    width = second.shape[1]
    edge_size = partner.shape[0]
    capacity = shape[0] // orbitals
    given = [] if relaid is None else [relaid]

    def kernel(edges_ref, second_ref, partner_ref, *refs):
        out_ref, window, block_rows, sem = refs[-4:]
        window[pl.ds(pl.multiple_of(edges_ref[1], 16), own * orbitals), :] = second_ref[...]
        window[pl.ds(pl.multiple_of(edges_ref[2], 16), edge_size), :] = partner_ref[...]
        for block in range(capacity):
            span = slice(block * orbitals, (block + 1) * orbitals)

            @pl.when(block < edges_ref[4])
            def _():
                row = pl.multiple_of(edges_ref[3] + block * orbitals, 16)
                block_rows[span, :] = window[pl.ds(row, orbitals), :]

            @pl.when(block >= edges_ref[4])
            def _():
                block_rows[span, :] = jnp.zeros((orbitals, width), block_rows.dtype)

        copy = pltpu.make_async_copy(block_rows, out_ref.at[:, pl.ds(low, width)], sem)
        copy.start()
        copy.wait()

    out = jax.ShapeDtypeStruct(shape, jnp.bfloat16)
    return pl.pallas_call(
        kernel,
        out_shape=out,
        in_specs=[SMEM] + [VMEM] * 2 + [HBM] * len(given),
        out_specs=HBM,
        scratch_shapes=[
            pltpu.VMEM((own * orbitals + edge_size, width), jnp.bfloat16),
            pltpu.VMEM((shape[0], width), jnp.bfloat16),
            pltpu.SemaphoreType.DMA,
        ],
        input_output_aliases={3: 0} if given else {},
        compiler_params=params(bytes_of(out) + 2 * bytes_of(second)),
        name="relaid_half",
    )(edges, second, partner, *given)


def ring_order(count):
    return [i for i in range(count) if i == 0 or i % 2] + [
        i for i in range(count - 1, 0, -1) if i and i % 2 == 0
    ]


def on_device(block_values, block_rows, block_cols, start_vectors, center, half_width, row_counts):
    orbitals = block_values.shape[-1]
    values = block_values.reshape(-1, orbitals, orbitals)
    row_ids = block_rows.reshape(-1)
    col_ids = block_cols.reshape(-1)
    entry_count = values.shape[0]
    own_rows, vec_count = start_vectors.shape
    own = own_rows // orbitals
    row_count = lax.axis_size("row")
    col_count = lax.axis_size("col")
    my_row = lax.axis_index("row")
    my_col = lax.axis_index("col")
    chip_count = col_count // 2

    order = ring_order(row_count)
    route = [(order[i], order[(i + 1) % row_count]) for i in range(row_count)]
    place_of = [order.index(i) for i in range(row_count)]

    def looked_up(table, index):
        result = jnp.zeros_like(index)
        for at, value in enumerate(table):
            result = jnp.where(index == at, value, result)
        return result

    half_blocks = own // 2
    capacity = own + half_blocks
    edge_size = half_blocks * orbitals
    parity = my_col % 2
    device = my_row * col_count + my_col
    even_count = row_counts[device - parity]
    edges = [
        (1 - parity) * (own_rows - edge_size),
        parity * edge_size,
        (1 - parity) * own_rows,
        parity * (even_count - (own - half_blocks)) * orbitals,
        row_counts[device],
    ]

    with jax.named_scope("entry_order"):
        arrival = lax.rem(
            looked_up(place_of, my_row) - looked_up(place_of, col_ids // own) + row_count, row_count
        )
        panel_cols = arrival * own + col_ids % own
        relative = (row_ids // own) ^ my_col
        piece = chip_count - 1 - relative // 2
        out_rows = (piece * 2 + 1 - relative % 2) * own + row_ids % own
        number = jnp.arange(entry_count, dtype=jnp.int32)
        is_last = (arrival == row_count - 1).astype(jnp.int32)
        key = is_last * (2 * chip_count * own) + out_rows
        before = (key[None, :] < key[:, None]) | (
            (key[None, :] == key[:, None]) & (number[None, :] < number[:, None])
        )
        rank = jnp.sum(before.astype(jnp.int32), 1)
        at_rank = rank[None, :] == number[:, None]

        def ordered(items):
            return jnp.sum(jnp.where(at_rank, items[None, :], 0), 1).astype(jnp.int32)

        room = (0, UNROLL)
        entry_order = jnp.pad(ordered(number), room)
        rows = jnp.pad(ordered(out_rows), room)
        cols = jnp.pad(ordered(panel_cols), room)
        bounds = jnp.stack([0, entry_count - jnp.sum(is_last), entry_count])
        bounds = jnp.concatenate([jnp.stack(edges), bounds]).astype(jnp.int32)
        tables = (bounds, entry_order, rows, cols)
    values = resident(values, tables)

    other_core = [(i, i ^ 1) for i in range(col_count)]
    lanes = 128 if vec_count % 128 == 0 else vec_count
    lows = list(range(0, vec_count, lanes))
    cut = own_rows // 2 if own_rows % 32 == 0 else own_rows
    sizes = [cut, own_rows - cut] if cut < own_rows else [own_rows]
    crossed = chip_count == 4 and len(sizes) == 2

    def along_row(array):
        return lax.ppermute(array, "row", route)

    def to_core(array):
        return lax.ppermute(array, "col", other_core)

    def to_chip(array, chip):
        return lax.ppermute(array, "col", [(i, i ^ 2 * chip) for i in range(col_count)])

    class Gather:
        def __init__(self, parts):
            self.arrived = [list(parts)]

        def step(self, ties):
            held = self.arrived[-1]
            if len(self.arrived) < row_count:
                self.arrived.append(
                    [along_row(tied(part, tie)) for part, tie in zip(held, ties)]
                )

    def tied(array, tokens):
        tokens = list(tokens)
        return lax.optimization_barrier((array, *tokens))[0] if tokens else array

    def terms_of(gather, following, tokens):
        none = [[] for _ in sizes]
        counts = (1, 3) if crossed else (1,) * chip_count
        parts = [part for step in gather.arrived[:-1] for part in step]
        parts[0] = tied(parts[0], tokens)
        early = early_images(2 * chip_count * own, tables, values, parts)
        last = gather.arrived[-1]
        outs = last_images(counts, (row_count - 1) * own, tables, values, early, last)

        def go_on(*ties):
            if following is not None:
                following.step(ties)

        if not crossed:
            kept = partner = None
            arrived = []
            for piece in range(chip_count):
                chip = chip_count - 1 - piece
                sent, kept = outs[2 * piece], outs[2 * piece + 1]
                partner = to_core(sent)
                if chip:
                    (both,) = summed([[(own_rows, [(kept, 0), (partner, 0)])]])
                    arrived.append(to_chip(both, chip))
            for _ in range(row_count):
                go_on(*none)
            low, terms = 0, []
            for size in sizes:
                pairs = [(array, low) for array in [kept, partner, *arrived]]
                terms.append((size, pairs))
                low += size
            return terms

        top, rest = sizes
        sent, kept, sent_others, others = outs
        if following is not None:
            sent = tied(sent, following.arrived[-1][:1])
        partner = to_core(sent)
        partners = to_core(tied(sent_others, [partner]))
        corner = summed(
            [[(top, [(kept, 0), (partner, 0)])], [(rest, [(kept, top), (partner, top)])]]
        )
        by_x, by_y = to_chip(corner[0], 1), to_chip(corner[1], 2)
        go_on([sent], corner)

        def both(low, *more):
            return [(others, low), (partners, low), *more]

        y, x, mine = 0, own_rows, 2 * own_rows
        sides = summed(
            [
                [(top, both(x)), (rest, both(x + top, (by_y, 0)))],
                [(top, both(y, (by_x, 0))), (rest, both(y + top))],
            ]
        )
        from_x, from_y = to_chip(sides[0], 1), to_chip(sides[1], 2)
        go_on(corner, sides)
        for _ in range(row_count):
            go_on(*none)
        return [
            (top, both(mine, (from_x, 0), (from_y, 0))),
            (rest, both(mine + top, (from_x, top), (from_y, top))),
        ]

    none = [[] for _ in sizes]
    gathers = []
    for low in lows:
        after = [[] for _ in sizes]
        if gathers:
            before = gathers[-1].arrived
            after = [[before[-2 if row_count > 1 else -1][i]] for i in range(len(sizes))]
        gather = Gather(
            columns_of(start_vectors, i * cut, size, low, lanes, after[i])
            for i, size in enumerate(sizes)
        )
        if not gathers:
            gather.step(none)
            gather.step([tables, *none[1:]])
            gather.step([*none[1:], [values]])
            for _ in range(row_count):
                gather.step(none)
        else:
            gather.step(none)
        gathers.append(gather)
    firsts = []
    count = len(lows)
    for turn in range(count):
        if turn:
            following = Gather(firsts[-1])
            following.step(none)
            gathers.append(following)
        following = gathers[turn + 1] if turn + 1 < len(gathers) else None
        terms = terms_of(gathers[turn], following, firsts[-1] if turn else [])
        firsts.append(first_update(terms, start_vectors, lows[turn], center, half_width))
    if count == 1:
        gathers.append(Gather(firsts[0]))
        for _ in range(row_count):
            gathers[-1].step(none)
    seconds = []
    relaid = None
    for turn in range(count):
        following = None
        if turn + 1 < count:
            if count + turn + 1 == len(gathers):
                gathers.append(Gather(firsts[turn + 1]))
                gathers[-1].step(none)
            following = gathers[count + turn + 1]
        tokens = seconds[-1:] if turn else firsts[-1]
        terms = terms_of(gathers[count + turn], following, tokens)
        if relaid is not None:
            size, ((array, row), *more) = terms[0]
            terms = [(size, [(tied(array, [relaid]), row), *more]), *terms[1:]]
        second, edge = second_update(
            terms, firsts[turn], start_vectors, lows[turn], center, half_width, tables, edge_size
        )
        seconds.append(second)
        shape = (capacity * orbitals, vec_count)
        relaid = relaid_half(
            relaid, second, to_core(edge), tables[0], lows[turn], shape, own, orbitals
        )
    return relaid


def solution(mesh):
    placed = (
        P("row", "col", None, None, None),
        P("row", "col", None),
        P("row", "col", None),
        P(("row", "col"), None),
        P(),
        P(),
        P(),
    )
    return jax.shard_map(
        on_device, mesh=mesh, in_specs=placed, out_specs=P(("row", "col"), None), check_vma=False
    )
```

```python
import functools
import math

import jax
import jax.numpy as jnp
from jax import lax
from jax.experimental import pallas as pl
from jax.experimental.pallas import tpu as pltpu
from jax.sharding import PartitionSpec as P

UNROLL = 32
EDGES = 5
MIB = 1 << 20
VMEM = pl.BlockSpec(memory_space=pltpu.VMEM)
SMEM = pl.BlockSpec(memory_space=pltpu.SMEM)
ANY = pl.BlockSpec(memory_space=pl.ANY)
HBM = pl.BlockSpec(memory_space=pltpu.HBM)


def bytes_of(*shapes):
    return sum(math.prod(s.shape) * jnp.dtype(s.dtype).itemsize for s in shapes)


def params(need):
    return pltpu.CompilerParams(vmem_limit_bytes=need + 3 * MIB)


def resident(values, after):
    def kernel(values_ref, *refs):
        held_ref, sem = refs[-2:]
        copy = pltpu.make_async_copy(values_ref, held_ref, sem)
        copy.start()
        copy.wait()

    return pl.pallas_call(
        kernel,
        out_shape=pltpu.VMEM(values.shape, values.dtype),
        in_specs=[HBM] + [ANY] * len(after),
        out_specs=VMEM,
        scratch_shapes=[pltpu.SemaphoreType.DMA],
        compiler_params=pltpu.CompilerParams(vmem_limit_bytes=MIB),
        cost_estimate=pl.CostEstimate(
            flops=0, bytes_accessed=bytes_of(values), transcendentals=0
        ),
        name="resident",
    )(values, *after)


def columns_of(vectors, row, rows, low, width, after):
    def kernel(vectors_ref, *refs):
        out_ref, sem = refs[-2:]
        copy = pltpu.make_async_copy(
            vectors_ref.at[pl.ds(row, rows), pl.ds(low, width)], out_ref, sem
        )
        copy.start()
        copy.wait()

    out = jax.ShapeDtypeStruct((rows, width), vectors.dtype)
    return pl.pallas_call(
        kernel,
        out_shape=out,
        in_specs=[HBM] + [ANY] * len(after),
        out_specs=VMEM,
        scratch_shapes=[pltpu.SemaphoreType.DMA],
        compiler_params=params(bytes_of(out)),
        cost_estimate=pl.CostEstimate(
            flops=0, bytes_accessed=2 * bytes_of(out), transcendentals=0
        ),
        name="columns_of",
    )(vectors, *after)


def rows_of(array, low, size):
    def kernel(array_ref, out_ref):
        out_ref[...] = array_ref[low : low + size, :]

    out = jax.ShapeDtypeStruct((size, array.shape[1]), array.dtype)
    return pl.pallas_call(
        kernel,
        out_shape=out,
        in_specs=[VMEM],
        out_specs=VMEM,
        compiler_params=params(bytes_of(array, out)),
        name="rows_of",
    )(array)


def add_images(bounds, order, rows, cols, values, panel, total, phase, low_col):
    orbitals = values.shape[-1]
    trash = total.shape[0] // orbitals - 1
    start = bounds[EDGES + phase]
    end = bounds[EDGES + phase + 1]

    def step(turn, carry):
        images = []
        for lane in range(UNROLL):
            entry = start + turn * UNROLL + lane
            col = jnp.where(entry < end, cols[entry] - low_col, 0)
            picked = panel[pl.ds(pl.multiple_of(col * orbitals, orbitals), orbitals), :]
            images.append(
                jnp.dot(values[order[entry]], picked, preferred_element_type=jnp.float32)
            )
        for lane in range(UNROLL):
            entry = start + turn * UNROLL + lane
            row = jnp.where(entry < end, rows[entry], trash)
            place = pl.ds(pl.multiple_of(row * orbitals, orbitals), orbitals)
            total[place, :] += images[lane]
        return carry

    lax.fori_loop(0, (end - start + UNROLL - 1) // UNROLL, step, 0)


def fill(panel, parts):
    low = 0
    for part in parts:
        panel[low : low + part.shape[0], :] = part[...]
        low += part.shape[0]


def early_images(out_blocks, tables, values, parts):
    orbitals = values.shape[-1]
    width = parts[0].shape[1]
    panel_rows = sum(part.shape[0] for part in parts)
    total = ((out_blocks + 1) * orbitals, width)

    def kernel(bounds, order, rows, cols, values, *refs):
        total_ref, panel = refs[-2:]
        fill(panel, refs[:-2])
        total_ref[...] = jnp.zeros_like(total_ref)
        add_images(bounds, order, rows, cols, values, panel, total_ref, 0, 0)

    return pl.pallas_call(
        kernel,
        out_shape=pltpu.VMEM(total, jnp.float32),
        in_specs=[SMEM] * 4 + [VMEM] * (1 + len(parts)),
        out_specs=VMEM,
        scratch_shapes=[pltpu.VMEM((panel_rows, width), jnp.bfloat16)],
        compiler_params=params(bytes_of(*parts, *parts)),
        name="early_images",
    )(*tables, values, *parts)


def last_images(counts, low_col, tables, values, early, parts):
    orbitals = values.shape[-1]
    width = parts[0].shape[1]
    panel_rows = sum(part.shape[0] for part in parts)
    height = (early.shape[0] - orbitals) // (2 * sum(counts))
    outs = [
        jax.ShapeDtypeStruct((count * height, width), jnp.bfloat16)
        for count in counts
        for _ in range(2)
    ]

    def kernel(bounds, order, rows, cols, values, early, *refs):
        part_refs, out_refs = refs[: len(parts)], refs[len(parts) + 1 : -1]
        total, panel = refs[len(parts)], refs[-1]
        fill(panel, part_refs)
        add_images(bounds, order, rows, cols, values, panel, total, 1, low_col)
        low = 0
        for count, *pair in zip(counts, out_refs[::2], out_refs[1::2]):
            for piece in range(count):
                for out in pair:
                    out[piece * height : (piece + 1) * height, :] = total[
                        low : low + height, :
                    ].astype(out.dtype)
                    low += height

    return pl.pallas_call(
        kernel,
        out_shape=[pltpu.VMEM(early.shape, jnp.float32), *outs],
        in_specs=[SMEM] * 4 + [VMEM] * (2 + len(parts)),
        out_specs=[VMEM] * (1 + len(outs)),
        scratch_shapes=[pltpu.VMEM((panel_rows, width), jnp.bfloat16)],
        input_output_aliases={5: 0},
        compiler_params=params(bytes_of(*parts, *parts, *outs)),
        name="last_images",
    )(*tables, values, early, *parts)[1:]


def summed(specs):
    flat = [array for segments in specs for _, pairs in segments for array, _ in pairs]

    def kernel(*refs):
        out_refs = refs[len(flat) :]
        at = 0
        for segments, out_ref in zip(specs, out_refs):
            row = 0
            for size, pairs in segments:
                total = image_rows(refs[at : at + len(pairs)], pairs, size)
                at += len(pairs)
                out_ref[row : row + size, :] = total.astype(out_ref.dtype)
                row += size

    width = flat[0].shape[1]
    outs = [
        jax.ShapeDtypeStruct((sum(size for size, _ in segments), width), flat[0].dtype)
        for segments in specs
    ]
    need = bytes_of(*flat, *outs)
    return pl.pallas_call(
        kernel,
        out_shape=outs,
        in_specs=[VMEM] * len(flat),
        out_specs=[VMEM] * len(outs),
        compiler_params=params(need),
        cost_estimate=pl.CostEstimate(flops=0, bytes_accessed=need, transcendentals=0),
        name="summed",
    )(*flat)


def image_rows(refs, pairs, size):
    image = None
    for ref, (_, low) in zip(refs, pairs):
        term = ref[low : low + size, :].astype(jnp.float32)
        image = term if image is None else image + term
    return image


def first_update(terms, vectors, low, center, half_width, top):
    flat = [array for _, pairs in terms for array, _ in pairs]
    width = flat[0].shape[1]

    def kernel(center_ref, width_ref, vectors_ref, *refs):
        full_ref, upper_ref, lower_ref = refs[len(flat) :]
        ((size, pairs),) = terms
        image = image_rows(refs[: len(flat)], pairs, size)
        source = vectors_ref[:, low : low + width].astype(jnp.float32)
        step = ((image - center_ref[0] * source) / width_ref[0]).astype(full_ref.dtype)
        full_ref[...] = step
        upper_ref[...] = step[:top]
        lower_ref[...] = step[top:]

    rows = terms[0][0]
    need = bytes_of(*flat, vectors)
    return pl.pallas_call(
        kernel,
        out_shape=[
            jax.ShapeDtypeStruct((size, width), jnp.bfloat16) for size in (rows, top, rows - top)
        ],
        in_specs=[SMEM] * 2 + [VMEM] * (1 + len(flat)),
        out_specs=[VMEM] * 3,
        compiler_params=params(need),
        cost_estimate=pl.CostEstimate(flops=0, bytes_accessed=need, transcendentals=0),
        name="first_update",
    )(center, half_width, vectors, *flat)


def second_update(terms, firsts, vectors, low, center, half_width, tables, edge_size):
    flat = [array for _, pairs in terms for array, _ in pairs]
    rows = sum(size for size, _ in terms)
    width = flat[0].shape[1]

    def kernel(edges_ref, center_ref, width_ref, vectors_ref, *refs):
        first_refs = refs[len(flat) : len(flat) + len(firsts)]
        out_ref, edge_ref = refs[-2:]
        row, at = 0, 0
        for (size, pairs), first_ref in zip(terms, first_refs):
            image = image_rows(refs[at : at + len(pairs)], pairs, size)
            at += len(pairs)
            source = vectors_ref[row : row + size, low : low + width].astype(jnp.float32)
            first = first_ref[...].astype(jnp.float32)
            out_ref[row : row + size, :] = (
                2.0 * (image - center_ref[0] * first) / width_ref[0] - source
            ).astype(out_ref.dtype)
            row += size
        edge_ref[...] = out_ref[pl.ds(pl.multiple_of(edges_ref[0], 16), edge_size), :]

    need = bytes_of(*flat, *firsts, vectors) + 4 * rows * width
    return pl.pallas_call(
        kernel,
        out_shape=[
            jax.ShapeDtypeStruct((rows, width), jnp.bfloat16),
            jax.ShapeDtypeStruct((edge_size, width), jnp.bfloat16),
        ],
        in_specs=[SMEM] * 3 + [VMEM] * (1 + len(flat) + len(firsts)),
        out_specs=[VMEM] * 2,
        compiler_params=params(need),
        cost_estimate=pl.CostEstimate(flops=0, bytes_accessed=need, transcendentals=0),
        name="second_update",
    )(tables[0], center, half_width, vectors, *flat, *firsts)


def relaid_half(relaid, second, partner, edges, low, shape, own, orbitals):
    width = second.shape[1]
    edge_size = partner.shape[0]
    capacity = shape[0] // orbitals
    given = [] if relaid is None else [relaid]

    def kernel(edges_ref, second_ref, partner_ref, *refs):
        out_ref, window, block_rows, sem = refs[-4:]
        window[pl.ds(pl.multiple_of(edges_ref[1], 16), own * orbitals), :] = second_ref[...]
        window[pl.ds(pl.multiple_of(edges_ref[2], 16), edge_size), :] = partner_ref[...]
        for block in range(capacity):
            span = slice(block * orbitals, (block + 1) * orbitals)

            @pl.when(block < edges_ref[4])
            def _():
                row = pl.multiple_of(edges_ref[3] + block * orbitals, 16)
                block_rows[span, :] = window[pl.ds(row, orbitals), :]

            @pl.when(block >= edges_ref[4])
            def _():
                block_rows[span, :] = jnp.zeros((orbitals, width), block_rows.dtype)

        copy = pltpu.make_async_copy(block_rows, out_ref.at[:, pl.ds(low, width)], sem)
        copy.start()
        copy.wait()

    out = jax.ShapeDtypeStruct(shape, jnp.bfloat16)
    return pl.pallas_call(
        kernel,
        out_shape=out,
        in_specs=[SMEM] + [VMEM] * 2 + [HBM] * len(given),
        out_specs=HBM,
        scratch_shapes=[
            pltpu.VMEM((own * orbitals + edge_size, width), jnp.bfloat16),
            pltpu.VMEM((shape[0], width), jnp.bfloat16),
            pltpu.SemaphoreType.DMA,
        ],
        input_output_aliases={3: 0} if given else {},
        compiler_params=params(bytes_of(out) + 2 * bytes_of(second)),
        name="relaid_half",
    )(edges, second, partner, *given)


def ring_order(count):
    return [i for i in range(count) if i == 0 or i % 2] + [
        i for i in range(count - 1, 0, -1) if i and i % 2 == 0
    ]


def on_device(block_values, block_rows, block_cols, start_vectors, center, half_width, row_counts):
    orbitals = block_values.shape[-1]
    values = block_values.reshape(-1, orbitals, orbitals)
    row_ids = block_rows.reshape(-1)
    col_ids = block_cols.reshape(-1)
    entry_count = values.shape[0]
    own_rows, vec_count = start_vectors.shape
    own = own_rows // orbitals
    row_count = lax.axis_size("row")
    col_count = lax.axis_size("col")
    my_row = lax.axis_index("row")
    my_col = lax.axis_index("col")
    chip_count = col_count // 2

    order = ring_order(row_count)
    route = [(order[i], order[(i + 1) % row_count]) for i in range(row_count)]
    place_of = [order.index(i) for i in range(row_count)]

    back_route = [(target, source) for source, target in route]
    both_ways = row_count == 4

    def looked_up(table, index):
        result = jnp.zeros_like(index)
        for at, value in enumerate(table):
            result = jnp.where(index == at, value, result)
        return result

    half_blocks = own // 2
    capacity = own + half_blocks
    edge_size = half_blocks * orbitals
    parity = my_col % 2
    device = my_row * col_count + my_col
    even_count = row_counts[device - parity]
    edges = [
        (1 - parity) * (own_rows - edge_size),
        parity * edge_size,
        (1 - parity) * own_rows,
        parity * (even_count - (own - half_blocks)) * orbitals,
        row_counts[device],
    ]

    with jax.named_scope("entry_order"):
        arrival = lax.rem(
            looked_up(place_of, my_row) - looked_up(place_of, col_ids // own) + row_count, row_count
        )
        if both_ways:
            arrival = looked_up([0, 1, 3, 2], arrival)
        panel_cols = arrival * own + col_ids % own
        relative = (row_ids // own) ^ my_col
        piece = chip_count - 1 - relative // 2
        out_rows = (piece * 2 + 1 - relative % 2) * own + row_ids % own
        number = jnp.arange(entry_count, dtype=jnp.int32)
        is_last = (arrival == row_count - 1).astype(jnp.int32)
        key = is_last * (2 * chip_count * own) + out_rows
        before = (key[None, :] < key[:, None]) | (
            (key[None, :] == key[:, None]) & (number[None, :] < number[:, None])
        )
        rank = jnp.sum(before.astype(jnp.int32), 1)
        at_rank = rank[None, :] == number[:, None]

        def ordered(items):
            return jnp.sum(jnp.where(at_rank, items[None, :], 0), 1).astype(jnp.int32)

        room = (0, UNROLL)
        entry_order = jnp.pad(ordered(number), room)
        rows = jnp.pad(ordered(out_rows), room)
        cols = jnp.pad(ordered(panel_cols), room)
        bounds = jnp.stack([0, entry_count - jnp.sum(is_last), entry_count])
        bounds = jnp.concatenate([jnp.stack(edges), bounds]).astype(jnp.int32)
        tables = (bounds, entry_order, rows, cols)
    values = resident(values, tables)

    other_core = [(i, i ^ 1) for i in range(col_count)]
    lanes = 128 if vec_count % 128 == 0 else vec_count
    lows = list(range(0, vec_count, lanes))
    top = own_rows // 32 * 16

    def to_core(array):
        return lax.ppermute(array, "col", other_core)

    def to_chip(array, chip):
        return lax.ppermute(array, "col", [(i, i ^ 2 * chip) for i in range(col_count)])

    def tied(array, tokens):
        tokens = list(tokens)
        return lax.optimization_barrier((array, *tokens))[0] if tokens else array

    class Gather:
        def __init__(self, part, upper, lower):
            if both_ways:
                upper, lower = (lax.ppermute(half, "row", route) for half in (upper, lower))
                self.early = [part, upper, lower, lax.ppermute(part, "row", back_route)]
            else:
                self.early = [part, lax.ppermute(part, "row", route)]

        def finish(self, tokens):
            self.send_last(tokens)
            self.images = early_images(2 * chip_count * own, tables, values, self.early)

        def send_last(self, tokens):
            if both_ways:
                _, upper, _, behind = self.early
                lower = rows_of(tied(behind, tokens), top, own_rows - top)
                self.last = [
                    lax.ppermute(tied(upper, tokens), "row", route),
                    lax.ppermute(lower, "row", back_route),
                ]
                return
            while len(self.early) < row_count:
                self.early.append(lax.ppermute(self.early[-1], "row", route))
            self.last = [self.early.pop()]

    def image_terms(gather, following, tokens):
        counts = (1, chip_count - 1) if chip_count > 1 else (1,)
        early = gather.images
        last = [tied(gather.last[0], tokens), *gather.last[1:]]
        outs = last_images(counts, (row_count - 1) * own, tables, values, early, last)
        pairs = []
        for sent, kept in zip(outs[::2], outs[1::2]):
            if pairs:
                sent = tied(sent, [pairs[-1][1]])
            elif following is not None and both_ways:
                sent = tied(sent, following.early[1:2])
            pairs.append((kept, to_core(sent)))
        terms, arrived, chip = [], [], chip_count - 1
        for count, (kept, partner) in zip(counts, pairs):
            places = [[(kept, i * own_rows), (partner, i * own_rows)] for i in range(count)]
            if chip < count:
                terms = places.pop()
            sums = summed([[(own_rows, place)] for place in places]) if places else []
            for array in sums:
                arrived.append((to_chip(array, chip), 0))
                chip -= 1
        if following is not None:
            following.finish(sums)
        return [(own_rows, [*terms, *arrived])]

    gathers = []
    for low in lows:
        after = [gathers[-1].images] if len(gathers) == 1 else []
        cuts = [(0, own_rows), (0, top), (top, own_rows - top)]
        gathers.append(
            Gather(*[columns_of(start_vectors, *cut, low, lanes, after) for cut in cuts])
        )
        if len(gathers) == 1:
            gathers[0].finish([*tables, values, gathers[0].early[2 if both_ways else 1]])
    firsts = []
    count = len(lows)
    for turn in range(count):
        if turn:
            gathers.append(Gather(*firsts[-1]))
        following = gathers[turn + 1] if turn + 1 < len(gathers) else None
        terms = image_terms(gathers[turn], following, firsts[-1] if turn else [])
        firsts.append(first_update(terms, start_vectors, lows[turn], center, half_width, top))
    if count == 1:
        gathers.append(Gather(*firsts[0]))
        gathers[-1].finish([])
    relaid = None
    seconds = []
    for turn in range(count):
        following = None
        if turn + 1 < count:
            if count + turn + 1 == len(gathers):
                gathers.append(Gather(*firsts[turn + 1]))
            following = gathers[count + turn + 1]
        tokens = seconds[-1:] if turn else firsts[-1]
        terms = image_terms(gathers[count + turn], following, tokens)
        if relaid is not None:
            ((size, ((array, row), *more)),) = terms
            terms = [(size, [(tied(array, [relaid]), row), *more])]
        second, edge = second_update(
            terms, firsts[turn][:1], start_vectors, lows[turn], center, half_width, tables, edge_size
        )
        seconds.append(second)
        shape = (capacity * orbitals, vec_count)
        relaid = relaid_half(
            relaid, second, to_core(edge), tables[0], lows[turn], shape, own, orbitals
        )
    return relaid


def solution(mesh):
    placed = (
        P("row", "col", None, None, None),
        P("row", "col", None),
        P("row", "col", None),
        P(("row", "col"), None),
        P(),
        P(),
        P(),
    )
    return jax.shard_map(
        on_device, mesh=mesh, in_specs=placed, out_specs=P(("row", "col"), None), check_vma=False
    )
```

```python
import functools
import math

import jax
import jax.numpy as jnp
from jax import lax
from jax.experimental import pallas as pl
from jax.experimental.pallas import tpu as pltpu
from jax.sharding import PartitionSpec as P

UNROLL = 32
EDGES = 5
MIB = 1 << 20
VMEM = pl.BlockSpec(memory_space=pltpu.VMEM)
SMEM = pl.BlockSpec(memory_space=pltpu.SMEM)
ANY = pl.BlockSpec(memory_space=pl.ANY)
HBM = pl.BlockSpec(memory_space=pltpu.HBM)


def bytes_of(*shapes):
    return sum(math.prod(s.shape) * jnp.dtype(s.dtype).itemsize for s in shapes)


def params(need):
    return pltpu.CompilerParams(vmem_limit_bytes=need + 3 * MIB)


def resident(values, after):
    def kernel(values_ref, *refs):
        held_ref, sem = refs[-2:]
        copy = pltpu.make_async_copy(values_ref, held_ref, sem)
        copy.start()
        copy.wait()

    return pl.pallas_call(
        kernel,
        out_shape=pltpu.VMEM(values.shape, values.dtype),
        in_specs=[HBM] + [ANY] * len(after),
        out_specs=VMEM,
        scratch_shapes=[pltpu.SemaphoreType.DMA],
        compiler_params=pltpu.CompilerParams(vmem_limit_bytes=MIB),
        cost_estimate=pl.CostEstimate(
            flops=0, bytes_accessed=bytes_of(values), transcendentals=0
        ),
        name="resident",
    )(values, *after)


def columns_of(vectors, row, rows, low, width, after):
    def kernel(vectors_ref, *refs):
        out_ref, sem = refs[-2:]
        copy = pltpu.make_async_copy(
            vectors_ref.at[pl.ds(row, rows), pl.ds(low, width)], out_ref, sem
        )
        copy.start()
        copy.wait()

    out = jax.ShapeDtypeStruct((rows, width), vectors.dtype)
    return pl.pallas_call(
        kernel,
        out_shape=out,
        in_specs=[HBM] + [ANY] * len(after),
        out_specs=VMEM,
        scratch_shapes=[pltpu.SemaphoreType.DMA],
        compiler_params=params(bytes_of(out)),
        cost_estimate=pl.CostEstimate(
            flops=0, bytes_accessed=2 * bytes_of(out), transcendentals=0
        ),
        name="columns_of",
    )(vectors, *after)


def rows_of(array, low, size):
    def kernel(array_ref, out_ref):
        out_ref[...] = array_ref[low : low + size, :]

    out = jax.ShapeDtypeStruct((size, array.shape[1]), array.dtype)
    return pl.pallas_call(
        kernel,
        out_shape=out,
        in_specs=[VMEM],
        out_specs=VMEM,
        compiler_params=params(bytes_of(array, out)),
        name="rows_of",
    )(array)


def add_images(bounds, order, rows, cols, values, panel, total, phase, low_col):
    orbitals = values.shape[-1]
    trash = total.shape[0] // orbitals - 1
    start = bounds[EDGES + phase]
    end = bounds[EDGES + phase + 1]

    def step(turn, carry):
        images = []
        for lane in range(UNROLL):
            entry = start + turn * UNROLL + lane
            col = jnp.where(entry < end, cols[entry] - low_col, 0)
            picked = panel[pl.ds(pl.multiple_of(col * orbitals, orbitals), orbitals), :]
            images.append(
                jnp.dot(values[order[entry]], picked, preferred_element_type=jnp.float32)
            )
        for lane in range(UNROLL):
            entry = start + turn * UNROLL + lane
            row = jnp.where(entry < end, rows[entry], trash)
            place = pl.ds(pl.multiple_of(row * orbitals, orbitals), orbitals)
            total[place, :] += images[lane]
        return carry

    lax.fori_loop(0, (end - start + UNROLL - 1) // UNROLL, step, 0)


def fill(panel, parts):
    low = 0
    for part in parts:
        panel[low : low + part.shape[0], :] = part[...]
        low += part.shape[0]


def early_images(out_blocks, tables, values, parts):
    orbitals = values.shape[-1]
    width = parts[0].shape[1]
    panel_rows = sum(part.shape[0] for part in parts)
    total = ((out_blocks + 1) * orbitals, width)

    def kernel(bounds, order, rows, cols, values, *refs):
        total_ref, panel = refs[-2:]
        fill(panel, refs[:-2])
        total_ref[...] = jnp.zeros_like(total_ref)
        add_images(bounds, order, rows, cols, values, panel, total_ref, 0, 0)

    return pl.pallas_call(
        kernel,
        out_shape=pltpu.VMEM(total, jnp.float32),
        in_specs=[SMEM] * 4 + [VMEM] * (1 + len(parts)),
        out_specs=VMEM,
        scratch_shapes=[pltpu.VMEM((panel_rows, width), jnp.bfloat16)],
        compiler_params=params(bytes_of(*parts, *parts)),
        name="early_images",
    )(*tables, values, *parts)


def last_images(counts, low_col, tables, values, early, parts):
    orbitals = values.shape[-1]
    width = parts[0].shape[1]
    panel_rows = sum(part.shape[0] for part in parts)
    height = (early.shape[0] - orbitals) // (2 * sum(counts))
    outs = [
        jax.ShapeDtypeStruct((count * height, width), jnp.bfloat16)
        for count in counts
        for _ in range(2)
    ]

    def kernel(bounds, order, rows, cols, values, early, *refs):
        part_refs, out_refs = refs[: len(parts)], refs[len(parts) + 1 : -1]
        total, panel = refs[len(parts)], refs[-1]
        fill(panel, part_refs)
        add_images(bounds, order, rows, cols, values, panel, total, 1, low_col)
        low = 0
        for count, *pair in zip(counts, out_refs[::2], out_refs[1::2]):
            for piece in range(count):
                for out in pair:
                    out[piece * height : (piece + 1) * height, :] = total[
                        low : low + height, :
                    ].astype(out.dtype)
                    low += height

    return pl.pallas_call(
        kernel,
        out_shape=[pltpu.VMEM(early.shape, jnp.float32), *outs],
        in_specs=[SMEM] * 4 + [VMEM] * (2 + len(parts)),
        out_specs=[VMEM] * (1 + len(outs)),
        scratch_shapes=[pltpu.VMEM((panel_rows, width), jnp.bfloat16)],
        input_output_aliases={5: 0},
        compiler_params=params(bytes_of(*parts, *parts, *outs)),
        name="last_images",
    )(*tables, values, early, *parts)[1:]


def summed(specs):
    flat = [array for segments in specs for _, pairs in segments for array, _ in pairs]

    def kernel(*refs):
        out_refs = refs[len(flat) :]
        at = 0
        for segments, out_ref in zip(specs, out_refs):
            row = 0
            for size, pairs in segments:
                total = image_rows(refs[at : at + len(pairs)], pairs, size)
                at += len(pairs)
                out_ref[row : row + size, :] = total.astype(out_ref.dtype)
                row += size

    width = flat[0].shape[1]
    outs = [
        jax.ShapeDtypeStruct((sum(size for size, _ in segments), width), flat[0].dtype)
        for segments in specs
    ]
    need = bytes_of(*flat, *outs)
    return pl.pallas_call(
        kernel,
        out_shape=outs,
        in_specs=[VMEM] * len(flat),
        out_specs=[VMEM] * len(outs),
        compiler_params=params(need),
        cost_estimate=pl.CostEstimate(flops=0, bytes_accessed=need, transcendentals=0),
        name="summed",
    )(*flat)


def image_rows(refs, pairs, size):
    image = None
    for ref, (_, low) in zip(refs, pairs):
        term = ref[low : low + size, :].astype(jnp.float32)
        image = term if image is None else image + term
    return image


def first_update(terms, vectors, low, center, half_width, top):
    flat = [array for _, pairs in terms for array, _ in pairs]
    width = flat[0].shape[1]

    def kernel(center_ref, width_ref, vectors_ref, *refs):
        full_ref, upper_ref, lower_ref = refs[len(flat) :]
        ((size, pairs),) = terms
        image = image_rows(refs[: len(flat)], pairs, size)
        source = vectors_ref[:, low : low + width].astype(jnp.float32)
        step = ((image - center_ref[0] * source) / width_ref[0]).astype(full_ref.dtype)
        full_ref[...] = step
        upper_ref[...] = step[:top]
        lower_ref[...] = step[top:]

    rows = terms[0][0]
    need = bytes_of(*flat, vectors)
    return pl.pallas_call(
        kernel,
        out_shape=[
            jax.ShapeDtypeStruct((size, width), jnp.bfloat16) for size in (rows, top, rows - top)
        ],
        in_specs=[SMEM] * 2 + [VMEM] * (1 + len(flat)),
        out_specs=[VMEM] * 3,
        compiler_params=params(need),
        cost_estimate=pl.CostEstimate(flops=0, bytes_accessed=need, transcendentals=0),
        name="first_update",
    )(center, half_width, vectors, *flat)


def second_update(terms, firsts, vectors, low, center, half_width, tables, edge_size):
    flat = [array for _, pairs in terms for array, _ in pairs]
    rows = sum(size for size, _ in terms)
    width = flat[0].shape[1]

    def kernel(edges_ref, center_ref, width_ref, vectors_ref, *refs):
        first_refs = refs[len(flat) : len(flat) + len(firsts)]
        out_ref, edge_ref = refs[-2:]
        row, at = 0, 0
        for (size, pairs), first_ref in zip(terms, first_refs):
            image = image_rows(refs[at : at + len(pairs)], pairs, size)
            at += len(pairs)
            source = vectors_ref[row : row + size, low : low + width].astype(jnp.float32)
            first = first_ref[...].astype(jnp.float32)
            out_ref[row : row + size, :] = (
                2.0 * (image - center_ref[0] * first) / width_ref[0] - source
            ).astype(out_ref.dtype)
            row += size
        edge_ref[...] = out_ref[pl.ds(pl.multiple_of(edges_ref[0], 16), edge_size), :]

    need = bytes_of(*flat, *firsts, vectors) + 4 * rows * width
    return pl.pallas_call(
        kernel,
        out_shape=[
            pltpu.VMEM((rows, width), jnp.bfloat16),
            jax.ShapeDtypeStruct((edge_size, width), jnp.bfloat16),
        ],
        in_specs=[SMEM] * 3 + [VMEM] * (1 + len(flat) + len(firsts)),
        out_specs=[VMEM] * 2,
        compiler_params=params(need),
        cost_estimate=pl.CostEstimate(flops=0, bytes_accessed=need, transcendentals=0),
        name="second_update",
    )(tables[0], center, half_width, vectors, *flat, *firsts)


def relaid_half(relaid, second, partner, edges, low, shape, own, orbitals):
    width = second.shape[1]
    edge_size = partner.shape[0]
    capacity = shape[0] // orbitals
    given = [] if relaid is None else [relaid]

    def kernel(edges_ref, second_ref, partner_ref, *refs):
        out_ref, window, block_rows, sem = refs[-4:]
        window[pl.ds(pl.multiple_of(edges_ref[1], 16), own * orbitals), :] = second_ref[...]
        window[pl.ds(pl.multiple_of(edges_ref[2], 16), edge_size), :] = partner_ref[...]
        for block in range(capacity):
            span = slice(block * orbitals, (block + 1) * orbitals)

            @pl.when(block < edges_ref[4])
            def _():
                row = pl.multiple_of(edges_ref[3] + block * orbitals, 16)
                block_rows[span, :] = window[pl.ds(row, orbitals), :]

            @pl.when(block >= edges_ref[4])
            def _():
                block_rows[span, :] = jnp.zeros((orbitals, width), block_rows.dtype)

        copy = pltpu.make_async_copy(block_rows, out_ref.at[:, pl.ds(low, width)], sem)
        copy.start()
        copy.wait()

    out = jax.ShapeDtypeStruct(shape, jnp.bfloat16)
    return pl.pallas_call(
        kernel,
        out_shape=out,
        in_specs=[SMEM] + [VMEM] * 2 + [HBM] * len(given),
        out_specs=HBM,
        scratch_shapes=[
            pltpu.VMEM((own * orbitals + edge_size, width), jnp.bfloat16),
            pltpu.VMEM((shape[0], width), jnp.bfloat16),
            pltpu.SemaphoreType.DMA,
        ],
        input_output_aliases={3: 0} if given else {},
        compiler_params=params(bytes_of(out) + 2 * bytes_of(second)),
        name="relaid_half",
    )(edges, second, partner, *given)


def ring_order(count):
    return [i for i in range(count) if i == 0 or i % 2] + [
        i for i in range(count - 1, 0, -1) if i and i % 2 == 0
    ]


def on_device(block_values, block_rows, block_cols, start_vectors, center, half_width, row_counts):
    orbitals = block_values.shape[-1]
    values = block_values.reshape(-1, orbitals, orbitals)
    row_ids = block_rows.reshape(-1)
    col_ids = block_cols.reshape(-1)
    entry_count = values.shape[0]
    own_rows, vec_count = start_vectors.shape
    own = own_rows // orbitals
    row_count = lax.axis_size("row")
    col_count = lax.axis_size("col")
    my_row = lax.axis_index("row")
    my_col = lax.axis_index("col")
    chip_count = col_count // 2

    order = ring_order(row_count)
    route = [(order[i], order[(i + 1) % row_count]) for i in range(row_count)]
    place_of = [order.index(i) for i in range(row_count)]

    back_route = [(target, source) for source, target in route]
    both_ways = row_count == 4

    def looked_up(table, index):
        result = jnp.zeros_like(index)
        for at, value in enumerate(table):
            result = jnp.where(index == at, value, result)
        return result

    half_blocks = own // 2
    capacity = own + half_blocks
    edge_size = half_blocks * orbitals
    parity = my_col % 2
    device = my_row * col_count + my_col
    even_count = row_counts[device - parity]
    edges = [
        (1 - parity) * (own_rows - edge_size),
        parity * edge_size,
        (1 - parity) * own_rows,
        parity * (even_count - (own - half_blocks)) * orbitals,
        row_counts[device],
    ]

    with jax.named_scope("entry_order"):
        arrival = lax.rem(
            looked_up(place_of, my_row) - looked_up(place_of, col_ids // own) + row_count, row_count
        )
        if both_ways:
            arrival = looked_up([0, 1, 3, 2], arrival)
        panel_cols = arrival * own + col_ids % own
        relative = (row_ids // own) ^ my_col
        piece = chip_count - 1 - relative // 2
        out_rows = (piece * 2 + 1 - relative % 2) * own + row_ids % own
        number = jnp.arange(entry_count, dtype=jnp.int32)
        is_last = (arrival == row_count - 1).astype(jnp.int32)
        key = is_last * (2 * chip_count * own) + out_rows
        before = (key[None, :] < key[:, None]) | (
            (key[None, :] == key[:, None]) & (number[None, :] < number[:, None])
        )
        rank = jnp.sum(before.astype(jnp.int32), 1)
        at_rank = rank[None, :] == number[:, None]

        def ordered(items):
            return jnp.sum(jnp.where(at_rank, items[None, :], 0), 1).astype(jnp.int32)

        room = (0, UNROLL)
        entry_order = jnp.pad(ordered(number), room)
        rows = jnp.pad(ordered(out_rows), room)
        cols = jnp.pad(ordered(panel_cols), room)
        bounds = jnp.stack([0, entry_count - jnp.sum(is_last), entry_count])
        bounds = jnp.concatenate([jnp.stack(edges), bounds]).astype(jnp.int32)
        tables = (bounds, entry_order, rows, cols)
    values = resident(values, tables)

    other_core = [(i, i ^ 1) for i in range(col_count)]
    lanes = 128 if vec_count % 128 == 0 else vec_count
    lows = list(range(0, vec_count, lanes))
    top = own_rows // 32 * 16

    def to_core(array):
        return lax.ppermute(array, "col", other_core)

    def to_chip(array, chip):
        return lax.ppermute(array, "col", [(i, i ^ 2 * chip) for i in range(col_count)])

    def tied(array, tokens):
        tokens = list(tokens)
        return lax.optimization_barrier((array, *tokens))[0] if tokens else array

    class Gather:
        def __init__(self, part, upper, lower):
            if both_ways:
                upper, lower = (lax.ppermute(half, "row", route) for half in (upper, lower))
                self.early = [part, upper, lower, lax.ppermute(part, "row", back_route)]
            else:
                self.early = [part, lax.ppermute(part, "row", route)]

        def finish(self, tokens):
            self.send_last(tokens)
            self.images = early_images(2 * chip_count * own, tables, values, self.early)

        def send_last(self, tokens):
            if both_ways:
                _, upper, _, behind = self.early
                lower = rows_of(tied(behind, tokens), top, own_rows - top)
                self.last = [
                    lax.ppermute(tied(upper, tokens), "row", route),
                    lax.ppermute(lower, "row", back_route),
                ]
                return
            while len(self.early) < row_count:
                self.early.append(lax.ppermute(self.early[-1], "row", route))
            self.last = [self.early.pop()]

    def crossed_terms(pairs):
        (kept, partner), (others, partners) = pairs
        rest = own_rows - top
        y, x, mine = 0, own_rows, 2 * own_rows

        def both(low, *more):
            return [(others, low), (partners, low), *more]

        corner = summed(
            [[(top, [(kept, 0), (partner, 0)])], [(rest, [(kept, top), (partner, top)])]]
        )
        by_x, by_y = to_chip(corner[0], 1), to_chip(corner[1], 2)
        sides = summed([[(top, both(x))], [(rest, both(y + top))]])
        x_top, y_rest = to_chip(sides[0], 1), to_chip(sides[1], 2)
        joined = summed(
            [[(rest, both(x + top, (by_y, 0)))], [(top, both(y, (by_x, 0)))]]
        )
        x_rest, y_top = to_chip(joined[0], 1), to_chip(joined[1], 2)
        return [
            (top, both(mine, (x_top, 0), (y_top, 0))),
            (rest, both(mine + top, (x_rest, 0), (y_rest, 0))),
        ]

    def image_terms(gather, following, tokens):
        counts = (1, chip_count - 1) if chip_count > 1 else (1,)
        early = gather.images
        last = [tied(gather.last[0], tokens), *gather.last[1:]]
        outs = last_images(counts, (row_count - 1) * own, tables, values, early, last)
        pairs = []
        for sent, kept in zip(outs[::2], outs[1::2]):
            if pairs:
                sent = tied(sent, [pairs[-1][1]])
            elif following is not None and both_ways:
                sent = tied(sent, following.early[1:2])
            pairs.append((kept, to_core(sent)))
        if following is None and chip_count == 4:
            return crossed_terms(pairs)
        terms, arrived, chip = [], [], chip_count - 1
        for count, (kept, partner) in zip(counts, pairs):
            places = [[(kept, i * own_rows), (partner, i * own_rows)] for i in range(count)]
            if chip < count:
                terms = places.pop()
            sums = summed([[(own_rows, place)] for place in places]) if places else []
            for array in sums:
                arrived.append((to_chip(array, chip), 0))
                chip -= 1
        if following is not None:
            following.finish(sums)
        return [(own_rows, [*terms, *arrived])]

    gathers = []
    for low in lows:
        after = [gathers[-1].images] if len(gathers) == 1 else []
        cuts = [(0, own_rows), (0, top), (top, own_rows - top)]
        gathers.append(
            Gather(*[columns_of(start_vectors, *cut, low, lanes, after) for cut in cuts])
        )
        if len(gathers) == 1:
            gathers[0].finish([*tables, values, gathers[0].early[2 if both_ways else 1]])
    firsts = []
    count = len(lows)
    for turn in range(count):
        if turn:
            gathers.append(Gather(*firsts[-1]))
        following = gathers[turn + 1] if turn + 1 < len(gathers) else None
        terms = image_terms(gathers[turn], following, firsts[-1] if turn else [])
        firsts.append(first_update(terms, start_vectors, lows[turn], center, half_width, top))
    if count == 1:
        gathers.append(Gather(*firsts[0]))
        gathers[-1].finish([])
    relaid = None
    seconds = []
    for turn in range(count):
        following = None
        if turn + 1 < count:
            if count + turn + 1 == len(gathers):
                gathers.append(Gather(*firsts[turn + 1]))
            following = gathers[count + turn + 1]
        tokens = seconds[-1:] if turn else firsts[-1]
        terms = image_terms(gathers[count + turn], following, tokens)
        if relaid is not None:
            (size, ((array, row), *more)), *others = terms
            terms = [(size, [(tied(array, [relaid]), row), *more]), *others]
        second, edge = second_update(
            terms, firsts[turn][len(terms) - 1 :][: len(terms)], start_vectors, lows[turn], center, half_width, tables, edge_size
        )
        seconds.append(second)
        shape = (capacity * orbitals, vec_count)
        relaid = relaid_half(
            relaid, second, to_core(edge), tables[0], lows[turn], shape, own, orbitals
        )
    return relaid


def solution(mesh):
    placed = (
        P("row", "col", None, None, None),
        P("row", "col", None),
        P("row", "col", None),
        P(("row", "col"), None),
        P(),
        P(),
        P(),
    )
    return jax.shard_map(
        on_device, mesh=mesh, in_specs=placed, out_specs=P(("row", "col"), None), check_vma=False
    )
```

```python
import functools
import math

import jax
import jax.numpy as jnp
from jax import lax
from jax.experimental import pallas as pl
from jax.experimental.pallas import tpu as pltpu
from jax.sharding import PartitionSpec as P

UNROLL = 32
EDGES = 5
MIB = 1 << 20
VMEM = pl.BlockSpec(memory_space=pltpu.VMEM)
SMEM = pl.BlockSpec(memory_space=pltpu.SMEM)
ANY = pl.BlockSpec(memory_space=pl.ANY)
HBM = pl.BlockSpec(memory_space=pltpu.HBM)


def bytes_of(*shapes):
    return sum(math.prod(s.shape) * jnp.dtype(s.dtype).itemsize for s in shapes)


def params(need):
    return pltpu.CompilerParams(vmem_limit_bytes=need + 3 * MIB)


def resident(values, after):
    def kernel(values_ref, *refs):
        held_ref, sem = refs[-2:]
        copy = pltpu.make_async_copy(values_ref, held_ref, sem)
        copy.start()
        copy.wait()

    return pl.pallas_call(
        kernel,
        out_shape=pltpu.VMEM(values.shape, values.dtype),
        in_specs=[HBM] + [ANY] * len(after),
        out_specs=VMEM,
        scratch_shapes=[pltpu.SemaphoreType.DMA],
        compiler_params=pltpu.CompilerParams(vmem_limit_bytes=MIB),
        cost_estimate=pl.CostEstimate(
            flops=0, bytes_accessed=bytes_of(values), transcendentals=0
        ),
        name="resident",
    )(values, *after)


def columns_of(vectors, row, rows, low, width, after):
    def kernel(vectors_ref, *refs):
        out_ref, sem = refs[-2:]
        copy = pltpu.make_async_copy(
            vectors_ref.at[pl.ds(row, rows), pl.ds(low, width)], out_ref, sem
        )
        copy.start()
        copy.wait()

    out = jax.ShapeDtypeStruct((rows, width), vectors.dtype)
    return pl.pallas_call(
        kernel,
        out_shape=out,
        in_specs=[HBM] + [ANY] * len(after),
        out_specs=VMEM,
        scratch_shapes=[pltpu.SemaphoreType.DMA],
        compiler_params=params(bytes_of(out)),
        cost_estimate=pl.CostEstimate(
            flops=0, bytes_accessed=2 * bytes_of(out), transcendentals=0
        ),
        name="columns_of",
    )(vectors, *after)


def rows_of(array, low, size):
    def kernel(array_ref, out_ref):
        out_ref[...] = array_ref[low : low + size, :]

    out = jax.ShapeDtypeStruct((size, array.shape[1]), array.dtype)
    return pl.pallas_call(
        kernel,
        out_shape=out,
        in_specs=[VMEM],
        out_specs=VMEM,
        compiler_params=params(bytes_of(array, out)),
        name="rows_of",
    )(array)


def add_images(bounds, order, rows, cols, values, panel, total, phase, low_col):
    orbitals = values.shape[-1]
    trash = total.shape[0] // orbitals - 1
    start = bounds[EDGES + phase]
    end = bounds[EDGES + phase + 1]

    def step(turn, carry):
        images = []
        for lane in range(UNROLL):
            entry = start + turn * UNROLL + lane
            col = jnp.where(entry < end, cols[entry] - low_col, 0)
            picked = panel[pl.ds(pl.multiple_of(col * orbitals, orbitals), orbitals), :]
            images.append(
                jnp.dot(values[order[entry]], picked, preferred_element_type=jnp.float32)
            )
        for lane in range(UNROLL):
            entry = start + turn * UNROLL + lane
            row = jnp.where(entry < end, rows[entry], trash)
            place = pl.ds(pl.multiple_of(row * orbitals, orbitals), orbitals)
            total[place, :] += images[lane]
        return carry

    lax.fori_loop(0, (end - start + UNROLL - 1) // UNROLL, step, 0)


def fill(panel, parts):
    low = 0
    for part in parts:
        panel[low : low + part.shape[0], :] = part[...]
        low += part.shape[0]


def early_images(out_blocks, tables, values, parts):
    orbitals = values.shape[-1]
    width = parts[0].shape[1]
    panel_rows = sum(part.shape[0] for part in parts)
    total = ((out_blocks + 1) * orbitals, width)

    def kernel(bounds, order, rows, cols, values, *refs):
        total_ref, panel = refs[-2:]
        fill(panel, refs[:-2])
        total_ref[...] = jnp.zeros_like(total_ref)
        add_images(bounds, order, rows, cols, values, panel, total_ref, 0, 0)

    return pl.pallas_call(
        kernel,
        out_shape=pltpu.VMEM(total, jnp.float32),
        in_specs=[SMEM] * 4 + [VMEM] * (1 + len(parts)),
        out_specs=VMEM,
        scratch_shapes=[pltpu.VMEM((panel_rows, width), jnp.bfloat16)],
        compiler_params=params(bytes_of(*parts, *parts)),
        name="early_images",
    )(*tables, values, *parts)


def middle_images(low_col, tables, values, early, parts):
    width = parts[0].shape[1]
    panel_rows = sum(part.shape[0] for part in parts)

    def kernel(bounds, order, rows, cols, values, early, *refs):
        total, panel = refs[-2:]
        fill(panel, refs[:-2])
        add_images(bounds, order, rows, cols, values, panel, total, 1, low_col)

    return pl.pallas_call(
        kernel,
        out_shape=pltpu.VMEM(early.shape, jnp.float32),
        in_specs=[SMEM] * 4 + [VMEM] * (2 + len(parts)),
        out_specs=VMEM,
        scratch_shapes=[pltpu.VMEM((panel_rows, width), jnp.bfloat16)],
        input_output_aliases={5: 0},
        compiler_params=params(bytes_of(*parts, *parts)),
        name="middle_images",
    )(*tables, values, early, *parts)


def last_images(counts, low_col, tables, values, early, parts):
    orbitals = values.shape[-1]
    width = parts[0].shape[1]
    panel_rows = sum(part.shape[0] for part in parts)
    height = (early.shape[0] - orbitals) // (2 * sum(counts))
    outs = [
        jax.ShapeDtypeStruct((count * height, width), jnp.bfloat16)
        for count in counts
        for _ in range(2)
    ]

    def kernel(bounds, order, rows, cols, values, early, *refs):
        part_refs, out_refs = refs[: len(parts)], refs[len(parts) + 1 : -1]
        total, panel = refs[len(parts)], refs[-1]
        fill(panel, part_refs)
        add_images(bounds, order, rows, cols, values, panel, total, 2, low_col)
        low = 0
        for count, *pair in zip(counts, out_refs[::2], out_refs[1::2]):
            for piece in range(count):
                for out in pair:
                    out[piece * height : (piece + 1) * height, :] = total[
                        low : low + height, :
                    ].astype(out.dtype)
                    low += height

    return pl.pallas_call(
        kernel,
        out_shape=[pltpu.VMEM(early.shape, jnp.float32), *outs],
        in_specs=[SMEM] * 4 + [VMEM] * (2 + len(parts)),
        out_specs=[VMEM] * (1 + len(outs)),
        scratch_shapes=[pltpu.VMEM((panel_rows, width), jnp.bfloat16)],
        input_output_aliases={5: 0},
        compiler_params=params(bytes_of(*parts, *parts, *outs)),
        name="last_images",
    )(*tables, values, early, *parts)[1:]


def summed(specs):
    flat = [array for segments in specs for _, pairs in segments for array, _ in pairs]

    def kernel(*refs):
        out_refs = refs[len(flat) :]
        at = 0
        for segments, out_ref in zip(specs, out_refs):
            row = 0
            for size, pairs in segments:
                total = image_rows(refs[at : at + len(pairs)], pairs, size)
                at += len(pairs)
                out_ref[row : row + size, :] = total.astype(out_ref.dtype)
                row += size

    width = flat[0].shape[1]
    outs = [
        jax.ShapeDtypeStruct((sum(size for size, _ in segments), width), flat[0].dtype)
        for segments in specs
    ]
    need = bytes_of(*flat, *outs)
    return pl.pallas_call(
        kernel,
        out_shape=outs,
        in_specs=[VMEM] * len(flat),
        out_specs=[VMEM] * len(outs),
        compiler_params=params(need),
        cost_estimate=pl.CostEstimate(flops=0, bytes_accessed=need, transcendentals=0),
        name="summed",
    )(*flat)


def image_rows(refs, pairs, size):
    image = None
    for ref, (_, low) in zip(refs, pairs):
        term = ref[low : low + size, :].astype(jnp.float32)
        image = term if image is None else image + term
    return image


def first_update(terms, vectors, low, center, half_width, top):
    flat = [array for _, pairs in terms for array, _ in pairs]
    width = flat[0].shape[1]

    def kernel(center_ref, width_ref, vectors_ref, *refs):
        full_ref, upper_ref, lower_ref = refs[len(flat) :]
        ((size, pairs),) = terms
        image = image_rows(refs[: len(flat)], pairs, size)
        source = vectors_ref[:, low : low + width].astype(jnp.float32)
        step = ((image - center_ref[0] * source) / width_ref[0]).astype(full_ref.dtype)
        full_ref[...] = step
        upper_ref[...] = step[:top]
        lower_ref[...] = step[top:]

    rows = terms[0][0]
    need = bytes_of(*flat, vectors)
    return pl.pallas_call(
        kernel,
        out_shape=[
            jax.ShapeDtypeStruct((size, width), jnp.bfloat16) for size in (rows, top, rows - top)
        ],
        in_specs=[SMEM] * 2 + [VMEM] * (1 + len(flat)),
        out_specs=[VMEM] * 3,
        compiler_params=params(need),
        cost_estimate=pl.CostEstimate(flops=0, bytes_accessed=need, transcendentals=0),
        name="first_update",
    )(center, half_width, vectors, *flat)


def second_update(terms, firsts, vectors, low, center, half_width, tables, edge_size):
    flat = [array for _, pairs in terms for array, _ in pairs]
    rows = sum(size for size, _ in terms)
    width = flat[0].shape[1]

    def kernel(edges_ref, center_ref, width_ref, vectors_ref, *refs):
        first_refs = refs[len(flat) : len(flat) + len(firsts)]
        out_ref, edge_ref = refs[-2:]
        row, at = 0, 0
        for (size, pairs), first_ref in zip(terms, first_refs):
            image = image_rows(refs[at : at + len(pairs)], pairs, size)
            at += len(pairs)
            source = vectors_ref[row : row + size, low : low + width].astype(jnp.float32)
            first = first_ref[...].astype(jnp.float32)
            out_ref[row : row + size, :] = (
                2.0 * (image - center_ref[0] * first) / width_ref[0] - source
            ).astype(out_ref.dtype)
            row += size
        edge_ref[...] = out_ref[pl.ds(pl.multiple_of(edges_ref[0], 16), edge_size), :]

    need = bytes_of(*flat, *firsts, vectors) + 4 * rows * width
    return pl.pallas_call(
        kernel,
        out_shape=[
            pltpu.VMEM((rows, width), jnp.bfloat16),
            jax.ShapeDtypeStruct((edge_size, width), jnp.bfloat16),
        ],
        in_specs=[SMEM] * 3 + [VMEM] * (1 + len(flat) + len(firsts)),
        out_specs=[VMEM] * 2,
        compiler_params=params(need),
        cost_estimate=pl.CostEstimate(flops=0, bytes_accessed=need, transcendentals=0),
        name="second_update",
    )(tables[0], center, half_width, vectors, *flat, *firsts)


def relaid_half(relaid, second, partner, edges, low, shape, own, orbitals):
    width = second.shape[1]
    edge_size = partner.shape[0]
    capacity = shape[0] // orbitals
    given = [] if relaid is None else [relaid]

    def kernel(edges_ref, second_ref, partner_ref, *refs):
        out_ref, window, block_rows, sem = refs[-4:]
        window[pl.ds(pl.multiple_of(edges_ref[1], 16), own * orbitals), :] = second_ref[...]
        window[pl.ds(pl.multiple_of(edges_ref[2], 16), edge_size), :] = partner_ref[...]
        for block in range(capacity):
            span = slice(block * orbitals, (block + 1) * orbitals)

            @pl.when(block < edges_ref[4])
            def _():
                row = pl.multiple_of(edges_ref[3] + block * orbitals, 16)
                block_rows[span, :] = window[pl.ds(row, orbitals), :]

            @pl.when(block >= edges_ref[4])
            def _():
                block_rows[span, :] = jnp.zeros((orbitals, width), block_rows.dtype)

        copy = pltpu.make_async_copy(block_rows, out_ref.at[:, pl.ds(low, width)], sem)
        copy.start()
        copy.wait()

    out = jax.ShapeDtypeStruct(shape, jnp.bfloat16)
    return pl.pallas_call(
        kernel,
        out_shape=out,
        in_specs=[SMEM] + [VMEM] * 2 + [HBM] * len(given),
        out_specs=HBM,
        scratch_shapes=[
            pltpu.VMEM((own * orbitals + edge_size, width), jnp.bfloat16),
            pltpu.VMEM((shape[0], width), jnp.bfloat16),
            pltpu.SemaphoreType.DMA,
        ],
        input_output_aliases={3: 0} if given else {},
        compiler_params=params(bytes_of(out) + 2 * bytes_of(second)),
        name="relaid_half",
    )(edges, second, partner, *given)


def ring_order(count):
    return [i for i in range(count) if i == 0 or i % 2] + [
        i for i in range(count - 1, 0, -1) if i and i % 2 == 0
    ]


def on_device(block_values, block_rows, block_cols, start_vectors, center, half_width, row_counts):
    orbitals = block_values.shape[-1]
    values = block_values.reshape(-1, orbitals, orbitals)
    row_ids = block_rows.reshape(-1)
    col_ids = block_cols.reshape(-1)
    entry_count = values.shape[0]
    own_rows, vec_count = start_vectors.shape
    own = own_rows // orbitals
    row_count = lax.axis_size("row")
    col_count = lax.axis_size("col")
    my_row = lax.axis_index("row")
    my_col = lax.axis_index("col")
    chip_count = col_count // 2

    order = ring_order(row_count)
    route = [(order[i], order[(i + 1) % row_count]) for i in range(row_count)]
    place_of = [order.index(i) for i in range(row_count)]

    back_route = [(target, source) for source, target in route]
    both_ways = row_count == 4

    def looked_up(table, index):
        result = jnp.zeros_like(index)
        for at, value in enumerate(table):
            result = jnp.where(index == at, value, result)
        return result

    half_blocks = own // 2
    capacity = own + half_blocks
    edge_size = half_blocks * orbitals
    parity = my_col % 2
    device = my_row * col_count + my_col
    even_count = row_counts[device - parity]
    edges = [
        (1 - parity) * (own_rows - edge_size),
        parity * edge_size,
        (1 - parity) * own_rows,
        parity * (even_count - (own - half_blocks)) * orbitals,
        row_counts[device],
    ]

    with jax.named_scope("entry_order"):
        arrival = lax.rem(
            looked_up(place_of, my_row) - looked_up(place_of, col_ids // own) + row_count, row_count
        )
        if both_ways:
            arrival = looked_up([0, 1, 3, 2], arrival)
        panel_cols = arrival * own + col_ids % own
        relative = (row_ids // own) ^ my_col
        piece = chip_count - 1 - relative // 2
        out_rows = (piece * 2 + 1 - relative % 2) * own + row_ids % own
        number = jnp.arange(entry_count, dtype=jnp.int32)
        is_own = (arrival == 0).astype(jnp.int32)
        is_last = (arrival == row_count - 1).astype(jnp.int32)
        key = (1 - is_own + is_last) * (2 * chip_count * own) + out_rows
        before = (key[None, :] < key[:, None]) | (
            (key[None, :] == key[:, None]) & (number[None, :] < number[:, None])
        )
        rank = jnp.sum(before.astype(jnp.int32), 1)
        at_rank = rank[None, :] == number[:, None]

        def ordered(items):
            return jnp.sum(jnp.where(at_rank, items[None, :], 0), 1).astype(jnp.int32)

        room = (0, UNROLL)
        entry_order = jnp.pad(ordered(number), room)
        rows = jnp.pad(ordered(out_rows), room)
        cols = jnp.pad(ordered(panel_cols), room)
        bounds = jnp.stack(
            [0, jnp.sum(is_own), entry_count - jnp.sum(is_last), entry_count]
        )
        bounds = jnp.concatenate([jnp.stack(edges), bounds]).astype(jnp.int32)
        tables = (bounds, entry_order, rows, cols)
    values = resident(values, tables)

    other_core = [(i, i ^ 1) for i in range(col_count)]
    lanes = 128 if vec_count % 128 == 0 else vec_count
    lows = list(range(0, vec_count, lanes))
    top = own_rows // 32 * 16

    def to_core(array):
        return lax.ppermute(array, "col", other_core)

    def to_chip(array, chip):
        return lax.ppermute(array, "col", [(i, i ^ 2 * chip) for i in range(col_count)])

    def tied(array, tokens):
        tokens = list(tokens)
        return lax.optimization_barrier((array, *tokens))[0] if tokens else array

    class Gather:
        def __init__(self, part, upper, lower):
            if both_ways:
                upper, lower = (lax.ppermute(half, "row", route) for half in (upper, lower))
                self.early = [part, upper, lower, lax.ppermute(part, "row", back_route)]
            else:
                self.early = [part, lax.ppermute(part, "row", route)]

        def finish(self, tokens):
            self.send_last(tokens)
            self.own_images = early_images(2 * chip_count * own, tables, values, self.early[:1])
            self.images = self.own_images
            if self.early[1:]:
                self.images = middle_images(own, tables, values, self.images, self.early[1:])

        def send_last(self, tokens):
            if both_ways:
                _, upper, _, behind = self.early
                lower = rows_of(tied(behind, tokens), top, own_rows - top)
                self.last = [
                    lax.ppermute(tied(upper, tokens), "row", route),
                    lax.ppermute(lower, "row", back_route),
                ]
                return
            while len(self.early) < row_count:
                self.early.append(lax.ppermute(self.early[-1], "row", route))
            self.last = [self.early.pop()]

    def crossed_terms(pairs):
        (kept, partner), (others, partners) = pairs
        rest = own_rows - top
        y, x, mine = 0, own_rows, 2 * own_rows

        def both(low, *more):
            return [(others, low), (partners, low), *more]

        corner = summed(
            [[(top, [(kept, 0), (partner, 0)])], [(rest, [(kept, top), (partner, top)])]]
        )
        by_x, by_y = to_chip(corner[0], 1), to_chip(corner[1], 2)
        sides = summed([[(top, both(x))], [(rest, both(y + top))]])
        x_top, y_rest = to_chip(sides[0], 1), to_chip(sides[1], 2)
        joined = summed(
            [[(rest, both(x + top, (by_y, 0)))], [(top, both(y, (by_x, 0)))]]
        )
        x_rest, y_top = to_chip(joined[0], 1), to_chip(joined[1], 2)
        return [
            (top, both(mine, (x_top, 0), (y_top, 0))),
            (rest, both(mine + top, (x_rest, 0), (y_rest, 0))),
        ]

    def image_terms(gather, following, tokens):
        counts = (1, chip_count - 1) if chip_count > 1 else (1,)
        early = gather.images
        last = [tied(gather.last[0], tokens), *gather.last[1:]]
        outs = last_images(counts, (row_count - 1) * own, tables, values, early, last)
        pairs = []
        for sent, kept in zip(outs[::2], outs[1::2]):
            if pairs:
                sent = tied(sent, [pairs[-1][1]])
            elif following is not None and both_ways:
                sent = tied(sent, following.early[1:2])
            pairs.append((kept, to_core(sent)))
        if following is None and chip_count == 4:
            return crossed_terms(pairs)
        terms, arrived, chip = [], [], chip_count - 1
        for count, (kept, partner) in zip(counts, pairs):
            places = [[(kept, i * own_rows), (partner, i * own_rows)] for i in range(count)]
            if chip < count:
                terms = places.pop()
            sums = summed([[(own_rows, place)] for place in places]) if places else []
            for array in sums:
                arrived.append((to_chip(array, chip), 0))
                chip -= 1
        if following is not None:
            following.finish(sums)
            (array, row), *terms = terms
            terms = [(tied(array, [following.own_images]), row), *terms]
        return [(own_rows, [*terms, *arrived])]

    gathers = []
    for low in lows:
        after = [gathers[-1].images] if len(gathers) == 1 else []
        cuts = [(0, own_rows), (0, top), (top, own_rows - top)]
        gathers.append(
            Gather(*[columns_of(start_vectors, *cut, low, lanes, after) for cut in cuts])
        )
        if len(gathers) == 1:
            gathers[0].finish([*tables, values, gathers[0].early[2 if both_ways else 1]])
    firsts = []
    count = len(lows)
    for turn in range(count):
        if turn:
            gathers.append(Gather(*firsts[-1]))
        following = gathers[turn + 1] if turn + 1 < len(gathers) else None
        terms = image_terms(gathers[turn], following, firsts[-1] if turn else [])
        firsts.append(first_update(terms, start_vectors, lows[turn], center, half_width, top))
    if count == 1:
        gathers.append(Gather(*firsts[0]))
        gathers[-1].finish([])
    relaid = None
    seconds = []
    for turn in range(count):
        following = None
        if turn + 1 < count:
            if count + turn + 1 == len(gathers):
                gathers.append(Gather(*firsts[turn + 1]))
            following = gathers[count + turn + 1]
        tokens = seconds[-1:] if turn else firsts[-1]
        terms = image_terms(gathers[count + turn], following, tokens)
        if relaid is not None:
            (size, ((array, row), *more)), *others = terms
            terms = [(size, [(tied(array, [relaid]), row), *more]), *others]
        second, edge = second_update(
            terms, firsts[turn][len(terms) - 1 :][: len(terms)], start_vectors, lows[turn], center, half_width, tables, edge_size
        )
        seconds.append(second)
        shape = (capacity * orbitals, vec_count)
        relaid = relaid_half(
            relaid, second, to_core(edge), tables[0], lows[turn], shape, own, orbitals
        )
    return relaid


def solution(mesh):
    placed = (
        P("row", "col", None, None, None),
        P("row", "col", None),
        P("row", "col", None),
        P(("row", "col"), None),
        P(),
        P(),
        P(),
    )
    return jax.shard_map(
        on_device, mesh=mesh, in_specs=placed, out_specs=P(("row", "col"), None), check_vma=False
    )
```

```python
import functools
import math

import jax
import jax.numpy as jnp
from jax import lax
from jax.experimental import pallas as pl
from jax.experimental.pallas import tpu as pltpu
from jax.sharding import PartitionSpec as P

UNROLL = 32
EDGES = 5
MIB = 1 << 20
VMEM = pl.BlockSpec(memory_space=pltpu.VMEM)
SMEM = pl.BlockSpec(memory_space=pltpu.SMEM)
ANY = pl.BlockSpec(memory_space=pl.ANY)
HBM = pl.BlockSpec(memory_space=pltpu.HBM)


def bytes_of(*shapes):
    return sum(math.prod(s.shape) * jnp.dtype(s.dtype).itemsize for s in shapes)


def params(need):
    return pltpu.CompilerParams(vmem_limit_bytes=need + 3 * MIB)


def resident(values, after):
    def kernel(values_ref, *refs):
        held_ref, sem = refs[-2:]
        copy = pltpu.make_async_copy(values_ref, held_ref, sem)
        copy.start()
        copy.wait()

    return pl.pallas_call(
        kernel,
        out_shape=pltpu.VMEM(values.shape, values.dtype),
        in_specs=[HBM] + [ANY] * len(after),
        out_specs=VMEM,
        scratch_shapes=[pltpu.SemaphoreType.DMA],
        compiler_params=pltpu.CompilerParams(vmem_limit_bytes=MIB),
        cost_estimate=pl.CostEstimate(
            flops=0, bytes_accessed=bytes_of(values), transcendentals=0
        ),
        name="resident",
    )(values, *after)


def columns_of(vectors, row, rows, low, width, after):
    def kernel(vectors_ref, *refs):
        out_ref, sem = refs[-2:]
        copy = pltpu.make_async_copy(
            vectors_ref.at[pl.ds(row, rows), pl.ds(low, width)], out_ref, sem
        )
        copy.start()
        copy.wait()

    out = jax.ShapeDtypeStruct((rows, width), vectors.dtype)
    return pl.pallas_call(
        kernel,
        out_shape=out,
        in_specs=[HBM] + [ANY] * len(after),
        out_specs=VMEM,
        scratch_shapes=[pltpu.SemaphoreType.DMA],
        compiler_params=params(bytes_of(out)),
        cost_estimate=pl.CostEstimate(
            flops=0, bytes_accessed=2 * bytes_of(out), transcendentals=0
        ),
        name="columns_of",
    )(vectors, *after)


def rows_of(array, low, size):
    def kernel(array_ref, out_ref):
        out_ref[...] = array_ref[low : low + size, :]

    out = jax.ShapeDtypeStruct((size, array.shape[1]), array.dtype)
    return pl.pallas_call(
        kernel,
        out_shape=out,
        in_specs=[VMEM],
        out_specs=VMEM,
        compiler_params=params(bytes_of(array, out)),
        name="rows_of",
    )(array)


def add_images(bounds, order, rows, cols, values, panel, total, phase, low_col):
    orbitals = values.shape[-1]
    trash = total.shape[0] // orbitals - 1
    start = bounds[EDGES + phase]
    end = bounds[EDGES + phase + 1]

    def step(turn, carry):
        images = []
        for lane in range(UNROLL):
            entry = start + turn * UNROLL + lane
            col = jnp.where(entry < end, cols[entry] - low_col, 0)
            picked = panel[pl.ds(pl.multiple_of(col * orbitals, orbitals), orbitals), :]
            images.append(
                jnp.dot(values[order[entry]], picked, preferred_element_type=jnp.float32)
            )
        for lane in range(UNROLL):
            entry = start + turn * UNROLL + lane
            row = jnp.where(entry < end, rows[entry], trash)
            place = pl.ds(pl.multiple_of(row * orbitals, orbitals), orbitals)
            total[place, :] += images[lane]
        return carry

    lax.fori_loop(0, (end - start + UNROLL - 1) // UNROLL, step, 0)


def fill(panel, parts):
    low = 0
    for part in parts:
        panel[low : low + part.shape[0], :] = part[...]
        low += part.shape[0]


def early_images(out_blocks, tables, values, parts):
    orbitals = values.shape[-1]
    width = parts[0].shape[1]
    panel_rows = sum(part.shape[0] for part in parts)
    total = ((out_blocks + 1) * orbitals, width)

    def kernel(bounds, order, rows, cols, values, *refs):
        total_ref, panel = refs[-2:]
        fill(panel, refs[:-2])
        total_ref[...] = jnp.zeros_like(total_ref)
        add_images(bounds, order, rows, cols, values, panel, total_ref, 0, 0)

    return pl.pallas_call(
        kernel,
        out_shape=pltpu.VMEM(total, jnp.float32),
        in_specs=[SMEM] * 4 + [VMEM] * (1 + len(parts)),
        out_specs=VMEM,
        scratch_shapes=[pltpu.VMEM((panel_rows, width), jnp.bfloat16)],
        compiler_params=params(bytes_of(*parts, *parts)),
        name="early_images",
    )(*tables, values, *parts)


def middle_images(low_col, tables, values, early, parts):
    width = parts[0].shape[1]
    panel_rows = sum(part.shape[0] for part in parts)

    def kernel(bounds, order, rows, cols, values, early, *refs):
        total, panel = refs[-2:]
        fill(panel, refs[:-2])
        add_images(bounds, order, rows, cols, values, panel, total, 1, low_col)

    return pl.pallas_call(
        kernel,
        out_shape=pltpu.VMEM(early.shape, jnp.float32),
        in_specs=[SMEM] * 4 + [VMEM] * (2 + len(parts)),
        out_specs=VMEM,
        scratch_shapes=[pltpu.VMEM((panel_rows, width), jnp.bfloat16)],
        input_output_aliases={5: 0},
        compiler_params=params(bytes_of(*parts, *parts)),
        name="middle_images",
    )(*tables, values, early, *parts)


def last_images(counts, low_col, tables, values, early, parts):
    orbitals = values.shape[-1]
    width = parts[0].shape[1]
    panel_rows = sum(part.shape[0] for part in parts)
    height = (early.shape[0] - orbitals) // (2 * sum(counts))
    outs = [
        jax.ShapeDtypeStruct((count * height, width), jnp.bfloat16)
        for count in counts
        for _ in range(2)
    ]

    def kernel(bounds, order, rows, cols, values, early, *refs):
        part_refs, out_refs = refs[: len(parts)], refs[len(parts) + 1 : -1]
        total, panel = refs[len(parts)], refs[-1]
        fill(panel, part_refs)
        add_images(bounds, order, rows, cols, values, panel, total, 2, low_col)
        low = 0
        for count, *pair in zip(counts, out_refs[::2], out_refs[1::2]):
            for piece in range(count):
                for out in pair:
                    out[piece * height : (piece + 1) * height, :] = total[
                        low : low + height, :
                    ].astype(out.dtype)
                    low += height

    return pl.pallas_call(
        kernel,
        out_shape=[pltpu.VMEM(early.shape, jnp.float32), *outs],
        in_specs=[SMEM] * 4 + [VMEM] * (2 + len(parts)),
        out_specs=[VMEM] * (1 + len(outs)),
        scratch_shapes=[pltpu.VMEM((panel_rows, width), jnp.bfloat16)],
        input_output_aliases={5: 0},
        compiler_params=params(bytes_of(*parts, *parts, *outs)),
        name="last_images",
    )(*tables, values, early, *parts)[1:]


def summed(specs):
    flat = [array for segments in specs for _, pairs in segments for array, _ in pairs]

    def kernel(*refs):
        out_refs = refs[len(flat) :]
        at = 0
        for segments, out_ref in zip(specs, out_refs):
            row = 0
            for size, pairs in segments:
                total = image_rows(refs[at : at + len(pairs)], pairs, size)
                at += len(pairs)
                out_ref[row : row + size, :] = total.astype(out_ref.dtype)
                row += size

    width = flat[0].shape[1]
    outs = [
        jax.ShapeDtypeStruct((sum(size for size, _ in segments), width), flat[0].dtype)
        for segments in specs
    ]
    need = bytes_of(*flat, *outs)
    return pl.pallas_call(
        kernel,
        out_shape=outs,
        in_specs=[VMEM] * len(flat),
        out_specs=[VMEM] * len(outs),
        compiler_params=params(need),
        cost_estimate=pl.CostEstimate(flops=0, bytes_accessed=need, transcendentals=0),
        name="summed",
    )(*flat)


def image_rows(refs, pairs, size):
    image = None
    for ref, (_, low) in zip(refs, pairs):
        term = ref[low : low + size, :].astype(jnp.float32)
        image = term if image is None else image + term
    return image


def first_update(terms, vectors, low, center, half_width, top):
    flat = [array for _, pairs in terms for array, _ in pairs]
    width = flat[0].shape[1]

    def kernel(center_ref, width_ref, vectors_ref, *refs):
        full_ref, upper_ref, lower_ref = refs[len(flat) :]
        ((size, pairs),) = terms
        image = image_rows(refs[: len(flat)], pairs, size)
        source = vectors_ref[:, low : low + width].astype(jnp.float32)
        step = ((image - center_ref[0] * source) / width_ref[0]).astype(full_ref.dtype)
        full_ref[...] = step
        upper_ref[...] = step[:top]
        lower_ref[...] = step[top:]

    rows = terms[0][0]
    need = bytes_of(*flat, vectors)
    return pl.pallas_call(
        kernel,
        out_shape=[
            jax.ShapeDtypeStruct((size, width), jnp.bfloat16) for size in (rows, top, rows - top)
        ],
        in_specs=[SMEM] * 2 + [VMEM] * (1 + len(flat)),
        out_specs=[VMEM] * 3,
        compiler_params=params(need),
        cost_estimate=pl.CostEstimate(flops=0, bytes_accessed=need, transcendentals=0),
        name="first_update",
    )(center, half_width, vectors, *flat)


def second_update(terms, firsts, vectors, low, center, half_width, tables, edge_size):
    flat = [array for _, pairs in terms for array, _ in pairs]
    rows = sum(size for size, _ in terms)
    width = flat[0].shape[1]

    def kernel(edges_ref, center_ref, width_ref, vectors_ref, *refs):
        first_refs = refs[len(flat) : len(flat) + len(firsts)]
        out_ref, edge_ref = refs[-2:]
        row, at = 0, 0
        for (size, pairs), first_ref in zip(terms, first_refs):
            image = image_rows(refs[at : at + len(pairs)], pairs, size)
            at += len(pairs)
            source = vectors_ref[row : row + size, low : low + width].astype(jnp.float32)
            first = first_ref[...].astype(jnp.float32)
            out_ref[row : row + size, :] = (
                2.0 * (image - center_ref[0] * first) / width_ref[0] - source
            ).astype(out_ref.dtype)
            row += size
        edge_ref[...] = out_ref[pl.ds(pl.multiple_of(edges_ref[0], 16), edge_size), :]

    need = bytes_of(*flat, *firsts, vectors) + 4 * rows * width
    return pl.pallas_call(
        kernel,
        out_shape=[
            pltpu.VMEM((rows, width), jnp.bfloat16),
            jax.ShapeDtypeStruct((edge_size, width), jnp.bfloat16),
        ],
        in_specs=[SMEM] * 3 + [VMEM] * (1 + len(flat) + len(firsts)),
        out_specs=[VMEM] * 2,
        compiler_params=params(need),
        cost_estimate=pl.CostEstimate(flops=0, bytes_accessed=need, transcendentals=0),
        name="second_update",
    )(tables[0], center, half_width, vectors, *flat, *firsts)


def relaid_half(relaid, second, partner, edges, low, shape, own, orbitals):
    width = second.shape[1]
    edge_size = partner.shape[0]
    capacity = shape[0] // orbitals
    given = [] if relaid is None else [relaid]

    def kernel(edges_ref, second_ref, partner_ref, *refs):
        out_ref, window, block_rows, sem = refs[-4:]
        window[pl.ds(pl.multiple_of(edges_ref[1], 16), own * orbitals), :] = second_ref[...]
        window[pl.ds(pl.multiple_of(edges_ref[2], 16), edge_size), :] = partner_ref[...]
        for block in range(capacity):
            span = slice(block * orbitals, (block + 1) * orbitals)

            @pl.when(block < edges_ref[4])
            def _():
                row = pl.multiple_of(edges_ref[3] + block * orbitals, 16)
                block_rows[span, :] = window[pl.ds(row, orbitals), :]

            @pl.when(block >= edges_ref[4])
            def _():
                block_rows[span, :] = jnp.zeros((orbitals, width), block_rows.dtype)

        copy = pltpu.make_async_copy(block_rows, out_ref.at[:, pl.ds(low, width)], sem)
        copy.start()
        copy.wait()

    out = jax.ShapeDtypeStruct(shape, jnp.bfloat16)
    return pl.pallas_call(
        kernel,
        out_shape=out,
        in_specs=[SMEM] + [VMEM] * 2 + [HBM] * len(given),
        out_specs=HBM,
        scratch_shapes=[
            pltpu.VMEM((own * orbitals + edge_size, width), jnp.bfloat16),
            pltpu.VMEM((shape[0], width), jnp.bfloat16),
            pltpu.SemaphoreType.DMA,
        ],
        input_output_aliases={3: 0} if given else {},
        compiler_params=params(bytes_of(out) + 2 * bytes_of(second)),
        name="relaid_half",
    )(edges, second, partner, *given)


def ring_order(count):
    return [i for i in range(count) if i == 0 or i % 2] + [
        i for i in range(count - 1, 0, -1) if i and i % 2 == 0
    ]


def on_device(block_values, block_rows, block_cols, start_vectors, center, half_width, row_counts):
    orbitals = block_values.shape[-1]
    values = block_values.reshape(-1, orbitals, orbitals)
    row_ids = block_rows.reshape(-1)
    col_ids = block_cols.reshape(-1)
    entry_count = values.shape[0]
    own_rows, vec_count = start_vectors.shape
    own = own_rows // orbitals
    row_count = lax.axis_size("row")
    col_count = lax.axis_size("col")
    my_row = lax.axis_index("row")
    my_col = lax.axis_index("col")
    chip_count = col_count // 2

    order = ring_order(row_count)
    route = [(order[i], order[(i + 1) % row_count]) for i in range(row_count)]
    place_of = [order.index(i) for i in range(row_count)]

    back_route = [(target, source) for source, target in route]
    both_ways = row_count == 4

    def looked_up(table, index):
        result = jnp.zeros_like(index)
        for at, value in enumerate(table):
            result = jnp.where(index == at, value, result)
        return result

    half_blocks = own // 2
    capacity = own + half_blocks
    edge_size = half_blocks * orbitals
    parity = my_col % 2
    device = my_row * col_count + my_col
    even_count = row_counts[device - parity]
    edges = [
        (1 - parity) * (own_rows - edge_size),
        parity * edge_size,
        (1 - parity) * own_rows,
        parity * (even_count - (own - half_blocks)) * orbitals,
        row_counts[device],
    ]

    with jax.named_scope("entry_order"):
        arrival = lax.rem(
            looked_up(place_of, my_row) - looked_up(place_of, col_ids // own) + row_count, row_count
        )
        if both_ways:
            arrival = looked_up([0, 1, 3, 2], arrival)
        panel_cols = arrival * own + col_ids % own
        relative = (row_ids // own) ^ my_col
        piece = chip_count - 1 - relative // 2
        out_rows = (piece * 2 + 1 - relative % 2) * own + row_ids % own
        number = jnp.arange(entry_count, dtype=jnp.int32)
        is_own = (arrival == 0).astype(jnp.int32)
        is_last = (arrival == row_count - 1).astype(jnp.int32)
        key = (1 - is_own + is_last) * (2 * chip_count * own) + out_rows
        before = (key[None, :] < key[:, None]) | (
            (key[None, :] == key[:, None]) & (number[None, :] < number[:, None])
        )
        rank = jnp.sum(before.astype(jnp.int32), 1)
        at_rank = rank[None, :] == number[:, None]

        def ordered(items):
            return jnp.sum(jnp.where(at_rank, items[None, :], 0), 1).astype(jnp.int32)

        room = (0, UNROLL)
        entry_order = jnp.pad(ordered(number), room)
        rows = jnp.pad(ordered(out_rows), room)
        cols = jnp.pad(ordered(panel_cols), room)
        bounds = jnp.stack(
            [0, jnp.sum(is_own), entry_count - jnp.sum(is_last), entry_count]
        )
        bounds = jnp.concatenate([jnp.stack(edges), bounds]).astype(jnp.int32)
        tables = (bounds, entry_order, rows, cols)
    values = resident(values, tables)

    other_core = [(i, i ^ 1) for i in range(col_count)]
    lanes = 128 if vec_count % 128 == 0 else vec_count
    lows = list(range(0, vec_count, lanes))
    top = own_rows // 32 * 16

    def to_core(array):
        return lax.ppermute(array, "col", other_core)

    def to_chip(array, chip):
        return lax.ppermute(array, "col", [(i, i ^ 2 * chip) for i in range(col_count)])

    def tied(array, tokens):
        tokens = list(tokens)
        return lax.optimization_barrier((array, *tokens))[0] if tokens else array

    class Gather:
        def __init__(self, part, upper, lower):
            if both_ways:
                upper, lower = (lax.ppermute(half, "row", route) for half in (upper, lower))
                self.early = [part, upper, lower, lax.ppermute(part, "row", back_route)]
            else:
                self.early = [part, lax.ppermute(part, "row", route)]

        def finish(self, tokens):
            self.send_last(tokens)
            self.own_images = early_images(2 * chip_count * own, tables, values, self.early[:1])
            self.images = self.own_images
            if self.early[1:]:
                self.images = middle_images(own, tables, values, self.images, self.early[1:])

        def send_last(self, tokens):
            if both_ways:
                _, upper, _, behind = self.early
                lower = rows_of(tied(behind, tokens), top, own_rows - top)
                self.last = [
                    lax.ppermute(tied(upper, tokens), "row", route),
                    lax.ppermute(lower, "row", back_route),
                ]
                return
            while len(self.early) < row_count:
                self.early.append(lax.ppermute(self.early[-1], "row", route))
            self.last = [self.early.pop()]

    def crossed_terms(pairs):
        (kept, partner), (others, partners) = pairs
        rest = own_rows - top
        y, x, mine = 0, own_rows, 2 * own_rows

        def both(low, *more):
            return [(others, low), (partners, low), *more]

        corner = summed(
            [[(top, [(kept, 0), (partner, 0)])], [(rest, [(kept, top), (partner, top)])]]
        )
        by_x, by_y = to_chip(corner[0], 1), to_chip(corner[1], 2)
        sides = summed([[(top, both(x))], [(rest, both(y + top))]])
        x_top, y_rest = to_chip(sides[0], 1), to_chip(sides[1], 2)
        by_y = tied(by_y, [x_top])
        joined = summed(
            [[(rest, both(x + top, (by_y, 0)))], [(top, both(y, (by_x, 0)))]]
        )
        x_rest, y_top = to_chip(joined[0], 1), to_chip(joined[1], 2)
        return [
            (top, both(mine, (x_top, 0), (y_top, 0))),
            (rest, both(mine + top, (x_rest, 0), (y_rest, 0))),
        ]

    def image_terms(gather, following, tokens):
        counts = (1, chip_count - 1) if chip_count > 1 else (1,)
        early = gather.images
        last = [tied(gather.last[0], tokens), *gather.last[1:]]
        outs = last_images(counts, (row_count - 1) * own, tables, values, early, last)
        pairs = []
        for sent, kept in zip(outs[::2], outs[1::2]):
            if pairs:
                sent = tied(sent, [pairs[-1][1]])
            elif following is not None and both_ways:
                sent = tied(sent, following.early[1:2])
            pairs.append((kept, to_core(sent)))
        if following is None and chip_count == 4:
            return crossed_terms(pairs)
        terms, arrived, chip = [], [], chip_count - 1
        for count, (kept, partner) in zip(counts, pairs):
            places = [[(kept, i * own_rows), (partner, i * own_rows)] for i in range(count)]
            if chip < count:
                terms = places.pop()
            sums = summed([[(own_rows, place)] for place in places]) if places else []
            for array in sums:
                arrived.append((to_chip(array, chip), 0))
                chip -= 1
        if following is not None:
            following.finish(sums)
            (array, row), *terms = terms
            terms = [(tied(array, [following.own_images]), row), *terms]
        return [(own_rows, [*terms, *arrived])]

    gathers = []
    for low in lows:
        after = [gathers[-1].images] if len(gathers) == 1 else []
        cuts = [(0, own_rows), (0, top), (top, own_rows - top)]
        gathers.append(
            Gather(*[columns_of(start_vectors, *cut, low, lanes, after) for cut in cuts])
        )
        if len(gathers) == 1:
            gathers[0].finish([*tables, values, gathers[0].early[2 if both_ways else 1]])
    firsts = []
    count = len(lows)
    for turn in range(count):
        if turn:
            gathers.append(Gather(*firsts[-1]))
        following = gathers[turn + 1] if turn + 1 < len(gathers) else None
        terms = image_terms(gathers[turn], following, firsts[-1] if turn else [])
        firsts.append(first_update(terms, start_vectors, lows[turn], center, half_width, top))
    if count == 1:
        gathers.append(Gather(*firsts[0]))
        gathers[-1].finish([])
    relaid = None
    seconds = []
    for turn in range(count):
        following = None
        if turn + 1 < count:
            if count + turn + 1 == len(gathers):
                gathers.append(Gather(*firsts[turn + 1]))
            following = gathers[count + turn + 1]
        tokens = seconds[-1:] if turn else firsts[-1]
        terms = image_terms(gathers[count + turn], following, tokens)
        if relaid is not None:
            (size, ((array, row), *more)), *others = terms
            terms = [(size, [(tied(array, [relaid]), row), *more]), *others]
        second, edge = second_update(
            terms, firsts[turn][len(terms) - 1 :][: len(terms)], start_vectors, lows[turn], center, half_width, tables, edge_size
        )
        seconds.append(second)
        shape = (capacity * orbitals, vec_count)
        relaid = relaid_half(
            relaid, second, to_core(edge), tables[0], lows[turn], shape, own, orbitals
        )
    return relaid


def solution(mesh):
    placed = (
        P("row", "col", None, None, None),
        P("row", "col", None),
        P("row", "col", None),
        P(("row", "col"), None),
        P(),
        P(),
        P(),
    )
    return jax.shard_map(
        on_device, mesh=mesh, in_specs=placed, out_specs=P(("row", "col"), None), check_vma=False
    )
```

```python
import functools
import math

import jax
import jax.numpy as jnp
from jax import lax
from jax.experimental import pallas as pl
from jax.experimental.pallas import tpu as pltpu
from jax.sharding import PartitionSpec as P

UNROLL = 32
EDGES = 5
MIB = 1 << 20
VMEM = pl.BlockSpec(memory_space=pltpu.VMEM)
SMEM = pl.BlockSpec(memory_space=pltpu.SMEM)
ANY = pl.BlockSpec(memory_space=pl.ANY)
HBM = pl.BlockSpec(memory_space=pltpu.HBM)


def bytes_of(*shapes):
    return sum(math.prod(s.shape) * jnp.dtype(s.dtype).itemsize for s in shapes)


def params(need):
    return pltpu.CompilerParams(vmem_limit_bytes=need + 3 * MIB)


def resident(values, after):
    def kernel(values_ref, *refs):
        held_ref, sem = refs[-2:]
        copy = pltpu.make_async_copy(values_ref, held_ref, sem)
        copy.start()
        copy.wait()

    return pl.pallas_call(
        kernel,
        out_shape=pltpu.VMEM(values.shape, values.dtype),
        in_specs=[HBM] + [ANY] * len(after),
        out_specs=VMEM,
        scratch_shapes=[pltpu.SemaphoreType.DMA],
        compiler_params=pltpu.CompilerParams(vmem_limit_bytes=MIB),
        cost_estimate=pl.CostEstimate(
            flops=0, bytes_accessed=bytes_of(values), transcendentals=0
        ),
        name="resident",
    )(values, *after)


def columns_of(vectors, row, rows, low, width, after):
    def kernel(vectors_ref, *refs):
        out_ref, sem = refs[-2:]
        copy = pltpu.make_async_copy(
            vectors_ref.at[pl.ds(row, rows), pl.ds(low, width)], out_ref, sem
        )
        copy.start()
        copy.wait()

    out = jax.ShapeDtypeStruct((rows, width), vectors.dtype)
    return pl.pallas_call(
        kernel,
        out_shape=out,
        in_specs=[HBM] + [ANY] * len(after),
        out_specs=VMEM,
        scratch_shapes=[pltpu.SemaphoreType.DMA],
        compiler_params=params(bytes_of(out)),
        cost_estimate=pl.CostEstimate(
            flops=0, bytes_accessed=2 * bytes_of(out), transcendentals=0
        ),
        name="columns_of",
    )(vectors, *after)


def rows_of(array, low, size):
    def kernel(array_ref, out_ref):
        out_ref[...] = array_ref[low : low + size, :]

    out = jax.ShapeDtypeStruct((size, array.shape[1]), array.dtype)
    return pl.pallas_call(
        kernel,
        out_shape=out,
        in_specs=[VMEM],
        out_specs=VMEM,
        compiler_params=params(bytes_of(array, out)),
        name="rows_of",
    )(array)


def add_images(bounds, order, rows, cols, values, panel, total, phase, low_col):
    orbitals = values.shape[-1]
    trash = total.shape[0] // orbitals - 1
    start = bounds[EDGES + phase]
    end = bounds[EDGES + phase + 1]

    def step(turn, carry):
        images = []
        for lane in range(UNROLL):
            entry = start + turn * UNROLL + lane
            col = jnp.where(entry < end, cols[entry] - low_col, 0)
            picked = panel[pl.ds(pl.multiple_of(col * orbitals, orbitals), orbitals), :]
            images.append(
                jnp.dot(values[order[entry]], picked, preferred_element_type=jnp.float32)
            )
        for lane in range(UNROLL):
            entry = start + turn * UNROLL + lane
            row = jnp.where(entry < end, rows[entry], trash)
            place = pl.ds(pl.multiple_of(row * orbitals, orbitals), orbitals)
            total[place, :] += images[lane]
        return carry

    lax.fori_loop(0, (end - start + UNROLL - 1) // UNROLL, step, 0)


def fill(panel, parts):
    low = 0
    for part in parts:
        panel[low : low + part.shape[0], :] = part[...]
        low += part.shape[0]


def early_images(out_blocks, tables, values, parts):
    orbitals = values.shape[-1]
    width = parts[0].shape[1]
    panel_rows = sum(part.shape[0] for part in parts)
    total = ((out_blocks + 1) * orbitals, width)

    def kernel(bounds, order, rows, cols, values, *refs):
        total_ref, panel = refs[-2:]
        fill(panel, refs[:-2])
        total_ref[...] = jnp.zeros_like(total_ref)
        add_images(bounds, order, rows, cols, values, panel, total_ref, 0, 0)

    return pl.pallas_call(
        kernel,
        out_shape=pltpu.VMEM(total, jnp.float32),
        in_specs=[SMEM] * 4 + [VMEM] * (1 + len(parts)),
        out_specs=VMEM,
        scratch_shapes=[pltpu.VMEM((panel_rows, width), jnp.bfloat16)],
        compiler_params=params(bytes_of(*parts, *parts)),
        name="early_images",
    )(*tables, values, *parts)


def middle_images(low_col, tables, values, early, parts):
    width = parts[0].shape[1]
    panel_rows = sum(part.shape[0] for part in parts)

    def kernel(bounds, order, rows, cols, values, early, *refs):
        total, panel = refs[-2:]
        fill(panel, refs[:-2])
        add_images(bounds, order, rows, cols, values, panel, total, 1, low_col)

    return pl.pallas_call(
        kernel,
        out_shape=pltpu.VMEM(early.shape, jnp.float32),
        in_specs=[SMEM] * 4 + [VMEM] * (2 + len(parts)),
        out_specs=VMEM,
        scratch_shapes=[pltpu.VMEM((panel_rows, width), jnp.bfloat16)],
        input_output_aliases={5: 0},
        compiler_params=params(bytes_of(*parts, *parts)),
        name="middle_images",
    )(*tables, values, early, *parts)


def last_images(counts, low_col, tables, values, early, parts):
    orbitals = values.shape[-1]
    width = parts[0].shape[1]
    panel_rows = sum(part.shape[0] for part in parts)
    height = (early.shape[0] - orbitals) // (2 * sum(counts))
    outs = [
        jax.ShapeDtypeStruct((count * height, width), jnp.bfloat16)
        for count in counts
        for _ in range(2)
    ]

    def kernel(bounds, order, rows, cols, values, early, *refs):
        part_refs, out_refs = refs[: len(parts)], refs[len(parts) + 1 : -1]
        total, panel = refs[len(parts)], refs[-1]
        fill(panel, part_refs)
        add_images(bounds, order, rows, cols, values, panel, total, 2, low_col)
        low = 0
        for count, *pair in zip(counts, out_refs[::2], out_refs[1::2]):
            for piece in range(count):
                for out in pair:
                    out[piece * height : (piece + 1) * height, :] = total[
                        low : low + height, :
                    ].astype(out.dtype)
                    low += height

    return pl.pallas_call(
        kernel,
        out_shape=[pltpu.VMEM(early.shape, jnp.float32), *outs],
        in_specs=[SMEM] * 4 + [VMEM] * (2 + len(parts)),
        out_specs=[VMEM] * (1 + len(outs)),
        scratch_shapes=[pltpu.VMEM((panel_rows, width), jnp.bfloat16)],
        input_output_aliases={5: 0},
        compiler_params=params(bytes_of(*parts, *parts, *outs)),
        name="last_images",
    )(*tables, values, early, *parts)[1:]


def summed(specs):
    flat = [array for segments in specs for _, pairs in segments for array, _ in pairs]

    def kernel(*refs):
        out_refs = refs[len(flat) :]
        at = 0
        for segments, out_ref in zip(specs, out_refs):
            row = 0
            for size, pairs in segments:
                total = image_rows(refs[at : at + len(pairs)], pairs, size)
                at += len(pairs)
                out_ref[row : row + size, :] = total.astype(out_ref.dtype)
                row += size

    width = flat[0].shape[1]
    outs = [
        jax.ShapeDtypeStruct((sum(size for size, _ in segments), width), flat[0].dtype)
        for segments in specs
    ]
    need = bytes_of(*flat, *outs)
    return pl.pallas_call(
        kernel,
        out_shape=outs,
        in_specs=[VMEM] * len(flat),
        out_specs=[VMEM] * len(outs),
        compiler_params=params(need),
        cost_estimate=pl.CostEstimate(flops=0, bytes_accessed=need, transcendentals=0),
        name="summed",
    )(*flat)


def image_rows(refs, pairs, size):
    image = None
    for ref, (_, low) in zip(refs, pairs):
        term = ref[low : low + size, :].astype(jnp.float32)
        image = term if image is None else image + term
    return image


def first_update(terms, vectors, low, center, half_width, top):
    flat = [array for _, pairs in terms for array, _ in pairs]
    width = flat[0].shape[1]

    def kernel(center_ref, width_ref, vectors_ref, *refs):
        full_ref, upper_ref, lower_ref = refs[len(flat) :]
        ((size, pairs),) = terms
        image = image_rows(refs[: len(flat)], pairs, size)
        source = vectors_ref[:, low : low + width].astype(jnp.float32)
        step = ((image - center_ref[0] * source) / width_ref[0]).astype(full_ref.dtype)
        full_ref[...] = step
        upper_ref[...] = step[:top]
        lower_ref[...] = step[top:]

    rows = terms[0][0]
    need = bytes_of(*flat, vectors)
    return pl.pallas_call(
        kernel,
        out_shape=[
            jax.ShapeDtypeStruct((size, width), jnp.bfloat16) for size in (rows, top, rows - top)
        ],
        in_specs=[SMEM] * 2 + [VMEM] * (1 + len(flat)),
        out_specs=[VMEM] * 3,
        compiler_params=params(need),
        cost_estimate=pl.CostEstimate(flops=0, bytes_accessed=need, transcendentals=0),
        name="first_update",
    )(center, half_width, vectors, *flat)


def second_update(terms, firsts, vectors, low, center, half_width, tables, edge_size):
    flat = [array for _, pairs in terms for array, _ in pairs]
    rows = sum(size for size, _ in terms)
    width = flat[0].shape[1]

    def kernel(edges_ref, center_ref, width_ref, vectors_ref, *refs):
        first_refs = refs[len(flat) : len(flat) + len(firsts)]
        out_ref, edge_ref = refs[-2:]
        row, at = 0, 0
        for (size, pairs), first_ref in zip(terms, first_refs):
            image = image_rows(refs[at : at + len(pairs)], pairs, size)
            at += len(pairs)
            source = vectors_ref[row : row + size, low : low + width].astype(jnp.float32)
            first = first_ref[...].astype(jnp.float32)
            out_ref[row : row + size, :] = (
                2.0 * (image - center_ref[0] * first) / width_ref[0] - source
            ).astype(out_ref.dtype)
            row += size
        edge_ref[...] = out_ref[pl.ds(pl.multiple_of(edges_ref[0], 16), edge_size), :]

    need = bytes_of(*flat, *firsts, vectors) + 4 * rows * width
    return pl.pallas_call(
        kernel,
        out_shape=[
            pltpu.VMEM((rows, width), jnp.bfloat16),
            jax.ShapeDtypeStruct((edge_size, width), jnp.bfloat16),
        ],
        in_specs=[SMEM] * 3 + [VMEM] * (1 + len(flat) + len(firsts)),
        out_specs=[VMEM] * 2,
        compiler_params=params(need),
        cost_estimate=pl.CostEstimate(flops=0, bytes_accessed=need, transcendentals=0),
        name="second_update",
    )(tables[0], center, half_width, vectors, *flat, *firsts)


def relaid_half(relaid, second, partner, edges, low, shape, own, orbitals):
    width = second.shape[1]
    edge_size = partner.shape[0]
    capacity = shape[0] // orbitals
    given = [] if relaid is None else [relaid]

    def kernel(edges_ref, second_ref, partner_ref, *refs):
        out_ref, window, block_rows, sems = refs[-4:]
        split = capacity // 2
        copies = []
        for index, (first, end) in enumerate([(0, split), (split, capacity)]):
            span = pl.ds(first * orbitals, (end - first) * orbitals)
            copies.append(
                pltpu.make_async_copy(
                    block_rows.at[span], out_ref.at[span, pl.ds(low, width)], sems.at[index]
                )
            )
        window[pl.ds(pl.multiple_of(edges_ref[1], 16), own * orbitals), :] = second_ref[...]
        window[pl.ds(pl.multiple_of(edges_ref[2], 16), edge_size), :] = partner_ref[...]
        for block in range(capacity):
            span = slice(block * orbitals, (block + 1) * orbitals)

            @pl.when(block < edges_ref[4])
            def _():
                row = pl.multiple_of(edges_ref[3] + block * orbitals, 16)
                block_rows[span, :] = window[pl.ds(row, orbitals), :]

            @pl.when(block >= edges_ref[4])
            def _():
                block_rows[span, :] = jnp.zeros((orbitals, width), block_rows.dtype)

            if block == split - 1:
                copies[0].start()

        copies[1].start()
        for copy in copies:
            copy.wait()

    out = jax.ShapeDtypeStruct(shape, jnp.bfloat16)
    return pl.pallas_call(
        kernel,
        out_shape=out,
        in_specs=[SMEM] + [VMEM] * 2 + [HBM] * len(given),
        out_specs=HBM,
        scratch_shapes=[
            pltpu.VMEM((own * orbitals + edge_size, width), jnp.bfloat16),
            pltpu.VMEM((shape[0], width), jnp.bfloat16),
            pltpu.SemaphoreType.DMA((2,)),
        ],
        input_output_aliases={3: 0} if given else {},
        compiler_params=params(bytes_of(out) + 2 * bytes_of(second)),
        name="relaid_half",
    )(edges, second, partner, *given)


def ring_order(count):
    return [i for i in range(count) if i == 0 or i % 2] + [
        i for i in range(count - 1, 0, -1) if i and i % 2 == 0
    ]


def on_device(block_values, block_rows, block_cols, start_vectors, center, half_width, row_counts):
    orbitals = block_values.shape[-1]
    values = block_values.reshape(-1, orbitals, orbitals)
    row_ids = block_rows.reshape(-1)
    col_ids = block_cols.reshape(-1)
    entry_count = values.shape[0]
    own_rows, vec_count = start_vectors.shape
    own = own_rows // orbitals
    row_count = lax.axis_size("row")
    col_count = lax.axis_size("col")
    my_row = lax.axis_index("row")
    my_col = lax.axis_index("col")
    chip_count = col_count // 2

    order = ring_order(row_count)
    route = [(order[i], order[(i + 1) % row_count]) for i in range(row_count)]
    place_of = [order.index(i) for i in range(row_count)]

    back_route = [(target, source) for source, target in route]
    both_ways = row_count == 4

    def looked_up(table, index):
        result = jnp.zeros_like(index)
        for at, value in enumerate(table):
            result = jnp.where(index == at, value, result)
        return result

    half_blocks = own // 2
    capacity = own + half_blocks
    edge_size = half_blocks * orbitals
    parity = my_col % 2
    device = my_row * col_count + my_col
    even_count = row_counts[device - parity]
    edges = [
        (1 - parity) * (own_rows - edge_size),
        parity * edge_size,
        (1 - parity) * own_rows,
        parity * (even_count - (own - half_blocks)) * orbitals,
        row_counts[device],
    ]

    with jax.named_scope("entry_order"):
        arrival = lax.rem(
            looked_up(place_of, my_row) - looked_up(place_of, col_ids // own) + row_count, row_count
        )
        if both_ways:
            arrival = looked_up([0, 1, 3, 2], arrival)
        panel_cols = arrival * own + col_ids % own
        relative = (row_ids // own) ^ my_col
        piece = chip_count - 1 - relative // 2
        out_rows = (piece * 2 + 1 - relative % 2) * own + row_ids % own
        number = jnp.arange(entry_count, dtype=jnp.int32)
        is_own = (arrival == 0).astype(jnp.int32)
        is_last = (arrival == row_count - 1).astype(jnp.int32)
        key = (1 - is_own + is_last) * (2 * chip_count * own) + out_rows
        before = (key[None, :] < key[:, None]) | (
            (key[None, :] == key[:, None]) & (number[None, :] < number[:, None])
        )
        rank = jnp.sum(before.astype(jnp.int32), 1)
        at_rank = rank[None, :] == number[:, None]

        def ordered(items):
            return jnp.sum(jnp.where(at_rank, items[None, :], 0), 1).astype(jnp.int32)

        room = (0, UNROLL)
        entry_order = jnp.pad(ordered(number), room)
        rows = jnp.pad(ordered(out_rows), room)
        cols = jnp.pad(ordered(panel_cols), room)
        bounds = jnp.stack(
            [0, jnp.sum(is_own), entry_count - jnp.sum(is_last), entry_count]
        )
        bounds = jnp.concatenate([jnp.stack(edges), bounds]).astype(jnp.int32)
        tables = (bounds, entry_order, rows, cols)
    values = resident(values, tables)

    other_core = [(i, i ^ 1) for i in range(col_count)]
    lanes = 128 if vec_count % 128 == 0 else vec_count
    lows = list(range(0, vec_count, lanes))
    top = own_rows // 32 * 16

    def to_core(array):
        return lax.ppermute(array, "col", other_core)

    def to_chip(array, chip):
        return lax.ppermute(array, "col", [(i, i ^ 2 * chip) for i in range(col_count)])

    def tied(array, tokens):
        tokens = list(tokens)
        return lax.optimization_barrier((array, *tokens))[0] if tokens else array

    class Gather:
        def __init__(self, part, upper, lower):
            if both_ways:
                upper, lower = (lax.ppermute(half, "row", route) for half in (upper, lower))
                self.early = [part, upper, lower, lax.ppermute(part, "row", back_route)]
            else:
                self.early = [part, lax.ppermute(part, "row", route)]

        def finish(self, tokens):
            self.send_last(tokens)
            self.own_images = early_images(2 * chip_count * own, tables, values, self.early[:1])
            self.images = self.own_images
            if self.early[1:]:
                self.images = middle_images(own, tables, values, self.images, self.early[1:])

        def send_last(self, tokens):
            if both_ways:
                _, upper, _, behind = self.early
                lower = rows_of(tied(behind, tokens), top, own_rows - top)
                self.last = [
                    lax.ppermute(tied(upper, tokens), "row", route),
                    lax.ppermute(lower, "row", back_route),
                ]
                return
            while len(self.early) < row_count:
                self.early.append(lax.ppermute(self.early[-1], "row", route))
            self.last = [self.early.pop()]

    def crossed_terms(pairs):
        (kept, partner), (others, partners) = pairs
        rest = own_rows - top
        y, x, mine = 0, own_rows, 2 * own_rows

        def both(low, *more):
            return [(others, low), (partners, low), *more]

        corner = summed(
            [[(top, [(kept, 0), (partner, 0)])], [(rest, [(kept, top), (partner, top)])]]
        )
        by_x, by_y = to_chip(corner[0], 1), to_chip(corner[1], 2)
        sides = summed([[(top, both(x))], [(rest, both(y + top))]])
        x_top, y_rest = to_chip(sides[0], 1), to_chip(sides[1], 2)
        joined = summed(
            [[(rest, both(x + top, (by_y, 0)))], [(top, both(y, (by_x, 0)))]]
        )
        x_rest, y_top = to_chip(joined[0], 1), to_chip(joined[1], 2)
        return [
            (top, both(mine, (x_top, 0), (y_top, 0))),
            (rest, both(mine + top, (x_rest, 0), (y_rest, 0))),
        ]

    def image_terms(gather, following, tokens):
        counts = (1, chip_count - 1) if chip_count > 1 else (1,)
        early = gather.images
        last = [tied(gather.last[0], tokens), *gather.last[1:]]
        outs = last_images(counts, (row_count - 1) * own, tables, values, early, last)
        pairs = []
        for sent, kept in zip(outs[::2], outs[1::2]):
            if pairs:
                sent = tied(sent, [pairs[-1][1]])
            elif following is not None and both_ways:
                sent = tied(sent, following.early[1:2])
            pairs.append((kept, to_core(sent)))
        if following is None and chip_count == 4:
            return crossed_terms(pairs)
        terms, arrived, chip = [], [], chip_count - 1
        for count, (kept, partner) in zip(counts, pairs):
            places = [[(kept, i * own_rows), (partner, i * own_rows)] for i in range(count)]
            if chip < count:
                terms = places.pop()
            sums = summed([[(own_rows, place)] for place in places]) if places else []
            for array in sums:
                arrived.append((to_chip(array, chip), 0))
                chip -= 1
        if following is not None:
            following.finish(sums)
            (array, row), *terms = terms
            terms = [(tied(array, [following.own_images]), row), *terms]
        return [(own_rows, [*terms, *arrived])]

    gathers = []
    for low in lows:
        after = [gathers[-1].images] if len(gathers) == 1 else []
        cuts = [(0, own_rows), (0, top), (top, own_rows - top)]
        gathers.append(
            Gather(*[columns_of(start_vectors, *cut, low, lanes, after) for cut in cuts])
        )
        if len(gathers) == 1:
            gathers[0].finish([*tables, values, gathers[0].early[2 if both_ways else 1]])
    firsts = []
    count = len(lows)
    for turn in range(count):
        if turn:
            gathers.append(Gather(*firsts[-1]))
        following = gathers[turn + 1] if turn + 1 < len(gathers) else None
        terms = image_terms(gathers[turn], following, firsts[-1] if turn else [])
        firsts.append(first_update(terms, start_vectors, lows[turn], center, half_width, top))
    if count == 1:
        gathers.append(Gather(*firsts[0]))
        gathers[-1].finish([])
    relaid = None
    seconds = []
    for turn in range(count):
        following = None
        if turn + 1 < count:
            if count + turn + 1 == len(gathers):
                gathers.append(Gather(*firsts[turn + 1]))
            following = gathers[count + turn + 1]
        tokens = seconds[-1:] if turn else firsts[-1]
        terms = image_terms(gathers[count + turn], following, tokens)
        if relaid is not None:
            (size, ((array, row), *more)), *others = terms
            terms = [(size, [(tied(array, [relaid]), row), *more]), *others]
        second, edge = second_update(
            terms, firsts[turn][len(terms) - 1 :][: len(terms)], start_vectors, lows[turn], center, half_width, tables, edge_size
        )
        seconds.append(second)
        shape = (capacity * orbitals, vec_count)
        relaid = relaid_half(
            relaid, second, to_core(edge), tables[0], lows[turn], shape, own, orbitals
        )
    return relaid


def solution(mesh):
    placed = (
        P("row", "col", None, None, None),
        P("row", "col", None),
        P("row", "col", None),
        P(("row", "col"), None),
        P(),
        P(),
        P(),
    )
    return jax.shard_map(
        on_device, mesh=mesh, in_specs=placed, out_specs=P(("row", "col"), None), check_vma=False
    )
```
